256 devices in a mesh: dp: 16 (over x, z_hi), expert: 16 (over y, z_lo, core).
Axes of the slice: x: 4, y: 4, z: 8 (z_hi: 4, z_lo: 2; z = z_hi * 2 + z_lo), core: 2. Of those that a mesh axis runs over, the one named last changes fastest.
Arguments:
- tokens: bfloat16 [65536, 2048], P(('dp', 'expert')), may hold values from -6 to 6
- cotangent: bfloat16 [65536, 2048], P(('dp', 'expert')), may hold values from -6 to 6
- route_ids: int32 [65536, 8], P(('dp', 'expert')), may hold values from 0 to 127, all different within a row
- route_weights: bfloat16 [65536, 8], P(('dp', 'expert')), may hold values from 0.25 to 1
- capacity: int32 [16], replicated, may hold values from 18 to 24, as said below
- old_owner: int32 [16], replicated, may hold values from 0 to 15, each once
- new_owner: int32 [16], replicated, may hold values from 0 to 15, each once
- w_gate: bfloat16 [16, 2048, 768], P('expert'), may hold values from -0.125 to 0.125
- w_up: bfloat16 [16, 2048, 768], P('expert'), may hold values from -0.125 to 0.125
- w_down: bfloat16 [16, 2048, 768], P('expert'), may hold values from -0.21875 to 0.21875
Outputs:
- grad_x: bfloat16 [65536, 2048], P(('dp', 'expert'))
- grad_weights: bfloat16 [65536, 8], P(('dp', 'expert'))
- grad_gate: bfloat16 [16, 2048, 768], P('expert', 'dp')
- grad_up: bfloat16 [16, 2048, 768], P('expert', 'dp')
- grad_down: bfloat16 [16, 2048, 768], P('expert', 'dp')
The draws below stay inside these ranges and needn't reach their ends.
Inputs may be any that keep to these rules, and one draw needn't show every extreme that they name: `route_ids`: each row names 8 different experts; every expert is named by some row. `old_owner`: each value once. `new_owner`: each value once. `capacity`: the value 24 is taken by some expert.
All inputs are finite; a program needn't handle non-finite values.
Results may differ from the reference program's by a relative error of at most 0.019.
Values may be sent and summed in bfloat16 or wider, within the bound.
A program may use at most 128 MiB of HBM per device.

```python
import math
import jax
import jax.numpy as jnp
from jax import lax

D = 2048
FFN = 768
TOK_DEV = 256
CAP = 24
TOPK = 8
EXPERTS = 16
ROUTED = 128
TOKENS = 65536
N_DP = 16
N_EXPERT = 16


def draw_capacity(key, part):
    key = jax.random.fold_in(key, 11)
    spread = jax.random.randint(key, (EXPERTS,), 3 * CAP // 4, CAP + 1)
    full_key = jax.random.fold_in(key, 5)
    full = jax.random.randint(full_key, (), 0, EXPERTS)
    return jnp.where(jnp.arange(EXPERTS) == full, CAP, spread).astype(jnp.int32)


def block_levels(stream_key, extent, split, low, largest):
    factor_of = 1.0
    for axis_at, blocks in split:
        steps = jax.random.uniform(jax.random.fold_in(jax.random.fold_in(stream_key, 6), axis_at), (blocks,), jnp.float32, low / len(split), largest / len(split))
        factor_of = factor_of * jnp.repeat(jnp.exp(steps), extent[axis_at] // blocks).reshape((-1,) + (1,) * (len(extent) - 1 - axis_at))
    return factor_of


def picks_of(stream_key, rows, number_of, top, lift):
    order = jax.random.permutation(jax.random.fold_in(stream_key, 1), number_of)
    favour = order
    for power in range(3):
        favour = favour * favour // number_of
    favour = favour * lift // number_of
    lots = jax.random.randint(jax.random.fold_in(stream_key, 2), (rows, number_of), 0, 4096) + favour
    holders = jax.random.permutation(jax.random.fold_in(stream_key, 3), rows)[jnp.arange(number_of) % rows]
    lots = jnp.where(jnp.arange(rows)[:, None] == holders[None, :], 1 << 14, lots)
    score = lots * number_of + jnp.arange(number_of)
    return lax.top_k(score.astype(jnp.int32), top)[1].astype(jnp.int32)


def scatter_about(stream_key, extent, scale, reach, split=(), kind=jnp.bfloat16):
    drawn = jax.random.normal(stream_key, extent, jnp.float32) * scale
    if len(split) > 0:
        drawn = block_levels(stream_key, extent, split, -0.22, 0.18) * drawn
    return jnp.clip(drawn, min=-reach, max=reach).astype(kind)


def setup_inputs(seed: int = 0) -> dict:
    splits = jax.random.split(jax.random.key(seed), 11)
    return {
        "tokens": scatter_about(splits[0], (TOKENS, D), 1.0, 6.0, ((0, 256),)),
        "cotangent": scatter_about(splits[1], (TOKENS, D), 1.0, 6.0, ((0, 256),)),
        "route_ids": picks_of(splits[2], TOKENS, ROUTED, TOPK, 1024),
        "route_weights": jnp.clip(jnp.exp(math.log(1.0) - 1.3862944 * jax.random.uniform(splits[3], (TOKENS, TOPK), jnp.float32) ** block_levels(splits[3], (TOKENS, TOPK), ((0, 256),), -0.2, 0.2)), 0.25, 1.0).astype(jnp.bfloat16),
        "capacity": draw_capacity(jax.random.fold_in(splits[10], 71), 0),
        "old_owner": jax.random.permutation(splits[5], EXPERTS).astype(jnp.int32),
        "new_owner": jax.random.permutation(splits[6], EXPERTS).astype(jnp.int32),
        "w_gate": scatter_about(splits[7], (EXPERTS, D, FFN), D ** -0.5, 0.125, ((0, 16),)),
        "w_up": scatter_about(splits[8], (EXPERTS, D, FFN), D ** -0.5, 0.125, ((0, 16),)),
        "w_down": scatter_about(splits[9], (EXPERTS, D, FFN), FFN ** -0.5, 0.21875, ((0, 16),)),
    }


def silu_slope(value):
    sigma = jax.nn.sigmoid(value)
    return sigma * (1.0 + value * (1.0 - sigma))

def reference(tokens, cotangent, route_ids, route_weights, capacity, old_owner, new_owner, w_gate, w_up, w_down):
    sources = N_DP * N_EXPERT
    width = tokens.shape[1]
    ranks = jnp.arange(EXPERTS, dtype=jnp.int32)
    local_ids = route_ids.reshape(sources, TOK_DEV * TOPK)
    chosen = (local_ids[:, :, None] == ranks[None, None, :]).astype(jnp.int32)
    before = jnp.cumsum(chosen, axis=1) - chosen
    position = lax.optimization_barrier(jnp.sum(before * chosen, axis=2))
    limit = lax.optimization_barrier(jnp.sum(chosen * capacity[None, None, :], axis=2))
    kept = position < limit
    source_rank = jnp.arange(sources, dtype=jnp.int32)[:, None]
    sentinel = TOKENS * TOPK
    dummy = EXPERTS * sources * CAP
    target = jnp.where(kept, (local_ids * sources + source_rank) * CAP + position, dummy)
    assignment = jnp.arange(sentinel, dtype=jnp.int32)
    table = jnp.full((dummy + 1,), sentinel, jnp.int32)
    table = table.at[target.reshape(-1)].set(assignment)
    table = table[:-1].reshape(EXPERTS, N_DP * N_EXPERT * CAP)
    tokens_pad = jnp.concatenate([tokens, jnp.zeros((1, width), tokens.dtype)], axis=0)
    cotangent_pad = jnp.concatenate([cotangent, jnp.zeros((1, width), cotangent.dtype)], axis=0)
    weights_pad = jnp.concatenate([route_weights.reshape(-1), jnp.zeros((1,), route_weights.dtype)], axis=0)
    grad_scale = 1.0 / math.sqrt(N_DP * N_EXPERT * CAP)
    contract_hidden = (((1,), (1,)), ((), ()))

    def by_row(block):
        return block.reshape(N_DP, N_EXPERT * CAP, -1).astype(jnp.float32)

    def per_expert(carry, expert):
        grad_acc, weight_acc = carry
        picks = table[expert]
        rows = picks // TOPK
        x_rows = tokens_pad[rows]
        c_rows = cotangent_pad[rows]
        w_rows = weights_pad[picks]
        slot = old_owner[expert]
        gate_w = w_gate[slot]
        up_w = w_up[slot]
        down_w = w_down[slot]
        gate = jnp.dot(x_rows, gate_w, preferred_element_type=jnp.float32)
        up = jnp.dot(x_rows, up_w, preferred_element_type=jnp.float32)
        act = jax.nn.silu(gate)
        hidden = (act * up).astype(jnp.bfloat16)
        out_rows = lax.dot_general(hidden, down_w, contract_hidden, preferred_element_type=jnp.float32)
        weight_slot = (lax.optimization_barrier(jnp.sum(out_rows * c_rows.astype(jnp.float32), axis=1)) / math.sqrt(width)).astype(jnp.bfloat16)
        scaled = (w_rows.astype(jnp.float32)[:, None] * c_rows.astype(jnp.float32)).astype(jnp.bfloat16)
        dhidden = jnp.dot(scaled, down_w, preferred_element_type=jnp.float32)
        dgate = (dhidden * up * silu_slope(gate)).astype(jnp.bfloat16)
        dup = (dhidden * act).astype(jnp.bfloat16)
        dx_rows = lax.dot_general(dgate, gate_w, contract_hidden, preferred_element_type=jnp.float32)
        dx_rows = dx_rows + lax.dot_general(dup, up_w, contract_hidden, preferred_element_type=jnp.float32)
        dx_rows = dx_rows.astype(jnp.bfloat16)
        grad_acc = grad_acc.at[rows].add(dx_rows.astype(jnp.float32))
        weight_acc = weight_acc.at[picks].add(weight_slot.astype(jnp.float32))
        x_blocks = by_row(x_rows)
        parts = jnp.stack([jnp.einsum('rnd,rnh->rdh', x_blocks, by_row(dgate)), jnp.einsum('rnd,rnh->rdh', x_blocks, by_row(dup)), jnp.einsum('rnd,rnh->rdh', by_row(scaled), by_row(hidden))], axis=0) * grad_scale
        partial_value = parts.astype(jnp.bfloat16)
        total = lax.optimization_barrier(jnp.sum(partial_value.astype(jnp.float32), axis=1)).astype(jnp.bfloat16)
        return ((grad_acc, weight_acc), total)
    start = (jnp.zeros((TOKENS + 1, width), jnp.float32), jnp.zeros((sentinel + 1,), jnp.float32))
    (grad_acc, weight_acc), expert_grads = lax.scan(per_expert, start, jnp.arange(EXPERTS, dtype=jnp.int32))
    grad_x = grad_acc[:TOKENS].astype(jnp.bfloat16)
    grad_weights = weight_acc[:sentinel].reshape(TOKENS, TOPK).astype(jnp.bfloat16)
    new_inverse = jnp.zeros((EXPERTS,), jnp.int32).at[new_owner].set(jnp.arange(EXPERTS, dtype=jnp.int32))
    placed = expert_grads[new_inverse]
    return (grad_x, grad_weights, placed[:, 0], placed[:, 1], placed[:, 2])
```

```python
import math

import jax
import jax.numpy as jnp
from jax import lax
from jax.experimental import pallas as pl
from jax.experimental.pallas import tpu as pltpu
from jax.sharding import PartitionSpec as P

MESH = pl.DeviceIdType.MESH
CAP = 24
LANES = 16
TOK = 256
D = 2048
FFN = 768
ROWS = LANES * CAP
PAIR = 2 * CAP
COLS = 256
CHUNKS = FFN // COLS
UNITS = 6 * CHUNKS
XBLK = D // 4
ZBLK = XBLK // 4
BF = jnp.bfloat16
F32 = jnp.float32
NT = (((1,), (1,)), ((), ()))


def iota(shape, dim):
    return lax.broadcasted_iota(jnp.int32, shape, dim)


def eye(n):
    return (iota((n, n), 0) == iota((n, n), 1)).astype(F32).astype(BF)


def dot(a, b):
    return jnp.dot(a, b, preferred_element_type=F32)


def dot_nt(a, b):
    return lax.dot_general(a, b, NT, preferred_element_type=F32)


def body(
    tok, cot, ids, rw, cap, old, old_s, new_s, wg_h, wu_h, wd_h,
    gx, gw, gg, gu, gd,
    wg, wu, wd, xs_send, xs_recv, xb, sb, hb, pb, xr, zb, zr,
    dx_send, dx_recv, ws_send, ws_recv, place_l, place_r, gbuf, p1a, p1b, p1c, p2, ob, wanted,
    w_sem, d_ss, d_rs, x_ss, x_rs, z_ss, z_rs, b_ss, b_rs, v_ss, v_rs, p_ss, p_rs, q_ss, q_rs,
):
    dp = lax.axis_index("dp")
    me = lax.axis_index("expert")
    x, zh = dp // 4, dp % 4
    y, zl, co = me // 4, (me // 2) % 2, me % 2
    p1 = (p1a, p1b, p1c)

    def at_x(s):
        return (((x + s + 4) % 4) * 4 + zh, me)

    def at_z(s):
        return (x * 4 + (zh + s + 4) % 4, me)

    def ahead(k):
        return ((y + k // 4) % 4) * 4 + ((zl + (k // 2) % 2) % 2) * 2 + (co + k % 2) % 2

    def behind(k):
        return ((y + 4 - k // 4) % 4) * 4 + ((zl + (k // 2) % 2) % 2) * 2 + (co + k % 2) % 2

    def remote(src, dst, ss, rs, device):
        return pltpu.make_async_remote_copy(
            src_ref=src, dst_ref=dst, send_sem=ss, recv_sem=rs,
            device_id=device, device_id_type=MESH,
        )

    def each_peer(step):
        def run(i, carry):
            step(LANES - i)
            return carry

        lax.fori_loop(1, LANES, run, 0)

    weights = [
        pltpu.make_async_copy(h.at[0], v, w_sem.at[i])
        for i, (h, v) in enumerate(((wg_h, wg), (wu_h, wu), (wd_h, wd)))
    ]
    for copy in weights:
        copy.start()
    barrier = pltpu.get_barrier_semaphore()

    def greet(k):
        pl.semaphore_signal(barrier, inc=1, device_id=(dp, ahead(k)), device_id_type=MESH)

    each_peer(greet)
    for s in (1, -1):
        pl.semaphore_signal(barrier, inc=1, device_id=at_x(s), device_id_type=MESH)
        pl.semaphore_signal(barrier, inc=1, device_id=at_z(s), device_id_type=MESH)

    ids_t = dot_nt(eye(8), ids[...].astype(F32).astype(BF))
    rw_t = dot_nt(eye(8), rw[...])
    mine = old[...] == iota((LANES, LANES), 0)
    ex = jnp.sum(jnp.where(mine, iota((LANES, LANES), 1), 0).astype(F32), axis=1, keepdims=True)
    limit = jnp.sum(jnp.where(mine, cap[...], 0).astype(F32), axis=1, keepdims=True)
    named = jnp.zeros((LANES, TOK), F32)
    w_sel = jnp.zeros((LANES, TOK), F32)
    for k in range(8):
        hit = ids_t[k : k + 1, :] == ex
        named = named + jnp.where(hit, 1.0, 0.0)
        w_sel = w_sel + jnp.where(hit, rw_t[k : k + 1, :], 0.0)
    earlier = (iota((TOK, TOK), 0) < iota((TOK, TOK), 1)).astype(F32).astype(BF)
    before = dot(named.astype(BF), earlier)
    pos = jnp.where((named > 0.5) & (before < limit), before, -1.0)
    p_of = iota((CAP, TOK), 0).astype(F32)
    nothing = jnp.zeros((CAP, TOK), F32)
    ones, weighted, left, right = [], [], [], []
    for s in range(LANES):
        one = jnp.where(pos[s : s + 1, :] == p_of, 1.0, 0.0)
        ones.append(one)
        weighted.append(one * w_sel[s : s + 1, :])
        left += [one, nothing]
        right += [nothing, one]
    place = jnp.concatenate(ones, axis=0).astype(BF)
    place_w = jnp.concatenate(weighted, axis=0).astype(BF)
    place_l[...] = jnp.concatenate(left, axis=0).astype(BF)
    place_r[...] = jnp.concatenate(right, axis=0).astype(BF)
    for c in range(D // 256):
        cols = slice(256 * c, 256 * c + 256)
        rows_x = dot(place, tok[:, cols])
        rows_s = dot(place_w, cot[:, cols])
        both = []
        for s in range(LANES):
            both += [rows_x[CAP * s : CAP * s + CAP], rows_s[CAP * s : CAP * s + CAP]]
        xs_send[:, cols] = jnp.concatenate(both, axis=0).astype(BF)

    pl.semaphore_wait(barrier, LANES - 1 + 4)

    def dispatch(k):
        to = ahead(k)
        return remote(
            xs_send.at[pl.ds(pl.multiple_of(PAIR * to, 16), PAIR)],
            xs_recv.at[pl.ds(pl.multiple_of(PAIR * k, 16), PAIR)],
            d_ss.at[k], d_rs.at[k], (dp, to),
        )

    each_peer(lambda k: dispatch(k).start())
    xs_recv[0:PAIR] = xs_send[pl.ds(pl.multiple_of(PAIR * me, 16), PAIR)]

    def look_up(j, carry):
        slot = jnp.int32(0)
        for n in range(LANES):
            slot = slot + jnp.where(new_s[n] == j, old_s[n], 0)
        wanted[j] = slot
        return carry

    lax.fori_loop(0, LANES, look_up, 0)
    for copy in weights:
        copy.wait()
    each_peer(lambda k: dispatch(k).wait_recv())

    for c in range(D // 256):
        cols = slice(256 * c, 256 * c + 256)
        both = xs_recv[:, cols].astype(F32)
        xb[:, cols] = jnp.concatenate(
            [both[PAIR * k : PAIR * k + CAP] for k in range(LANES)], axis=0
        ).astype(BF)
        sb[:, cols] = jnp.concatenate(
            [both[PAIR * k + CAP : PAIR * k + PAIR] for k in range(LANES)], axis=0
        ).astype(BF)

    def hidden_chunk(c, ws):
        cols = slice(COLS * c, COLS * c + COLS)
        gate = dot(xb[...], wg[:, cols])
        up = dot(xb[...], wu[:, cols])
        dh = dot(sb[...], wd[:, cols])
        sig = 1.0 / (1.0 + jnp.exp(-gate))
        act = gate * sig
        hidden = (act * up).astype(BF)
        hb[2, :, cols] = hidden
        hb[0, :, cols] = (dh * up * (sig * (1.0 + gate * (1.0 - sig)))).astype(BF)
        hb[1, :, cols] = (dh * act).astype(BF)
        return ws + jnp.sum(hidden.astype(F32) * dh, axis=1, keepdims=True)

    scale = 1.0 / math.sqrt(4 * 4 * LANES * CAP)

    def sign(u):
        return 1 if u % 2 == 0 else -1

    def x_block(u, k):
        return (x - sign(u) * (1 + k) + 8) % 4

    def z_block(u, k):
        return (zh - sign(u) * (1 + k) + 8) % 4

    def x_copy(u, k):
        return remote(
            pb.at[u, x_block(u, k)], xr.at[k, u], x_ss.at[k, u], x_rs.at[k, u], at_x(sign(u))
        )

    def z_copy(u, k):
        return remote(
            zb.at[u, z_block(u, k)], zr.at[k, u], z_ss.at[k, u], z_rs.at[k, u], at_z(sign(u))
        )

    def units_of(j):
        return (2 * j, 2 * j + 1)

    def product(j):
        c, m = j // 3, j % 3
        turned = hb[m, :, COLS * c : COLS * c + COLS].astype(F32).T.astype(BF)
        rows = sb if m == 2 else xb
        for q in range(4):
            part = (dot(turned, rows[:, XBLK * q : XBLK * q + XBLK]) * scale).astype(BF)
            for h, u in enumerate(units_of(j)):
                pb[u, q] = part[128 * h : 128 * h + 128]
        for u in units_of(j):
            x_copy(u, 0).start()

    def x_step(j, k):
        for u in units_of(j):
            x_copy(u, k - 1).wait_recv()
            b = x_block(u, k)
            pb[u, b] = (pb[u, b].astype(F32) + xr[k - 1, u].astype(F32)).astype(BF)
            x_copy(u, k).start()
            x_copy(u, k - 1).wait_send()

    def x_last(j):
        for u in units_of(j):
            x_copy(u, 2).wait_recv()
            total = (pb[u, x].astype(F32) + xr[2, u].astype(F32)).astype(BF)
            for q in range(4):
                zb[u, q] = total[:, ZBLK * q : ZBLK * q + ZBLK]
            z_copy(u, 0).start()
            x_copy(u, 2).wait_send()

    def z_step(j, k):
        for u in units_of(j):
            z_copy(u, k - 1).wait_recv()
            b = z_block(u, k)
            zb[u, b] = (zb[u, b].astype(F32) + zr[k - 1, u].astype(F32)).astype(BF)
            z_copy(u, k).start()
            z_copy(u, k - 1).wait_send()

    def z_last(j):
        for u in units_of(j):
            z_copy(u, 2).wait_recv()
            total = zb[u, zh].astype(F32) + zr[2, u].astype(F32)
            gbuf[u // 6, u % 6] = total.T.astype(BF)
            z_copy(u, 2).wait_send()

    def piece(n):
        return pl.ds(3 * (n % 2), 3), pl.ds(pl.multiple_of(16 * (n // 2), 16), 16)

    def out_copy(g, k):
        to = ahead(k)
        us, rs = piece(to)
        return remote(
            gbuf.at[g, us, rs], p1[g].at[me], p_ss.at[g, k], p_rs.at[g, k], (dp, to)
        )

    def in_copy(g, k):
        to = ahead(k)
        us, rs = piece(me)
        return remote(p2.at[g, to], ob.at[g, us, rs], q_ss.at[g, k], q_rs.at[g, k], (dp, to))

    def move_out(g):
        each_peer(lambda k: out_copy(g, k).start())
        us, rs = piece(me)
        p1[g][me] = gbuf[g, us, rs]

    def move_pick(g):
        each_peer(lambda k: out_copy(g, k).wait_recv())

        def pick(j, carry):
            p2[g, j] = p1[g][wanted[j]]
            return carry

        lax.fori_loop(0, LANES, pick, 0)
        each_peer(lambda k: in_copy(g, k).start())
        us, rs = piece(me)
        ob[g, us, rs] = p2[g, me]
        each_peer(lambda k: out_copy(g, k).wait_send())

    def move_in(g):
        each_peer(lambda k: in_copy(g, k).wait_recv())
        for m, out in enumerate((gg, gu, gd)):
            for h in range(2):
                at = COLS * g + 128 * h
                out[0, :, at : at + 128] = ob[g, 2 * m + h]
        each_peer(lambda k: in_copy(g, k).wait_send())

    def back_copy(k):
        to = behind(k)
        return remote(
            dx_send.at[pl.ds(pl.multiple_of(PAIR * k, 16), PAIR)],
            dx_recv.at[pl.ds(pl.multiple_of(PAIR * me, 16), PAIR)],
            b_ss.at[k], b_rs.at[k], (dp, to),
        )

    def value_copy(k):
        return remote(ws_send.at[k], ws_recv.at[me], v_ss.at[k], v_rs.at[k], (dp, behind(k)))

    diagonal = iota((CAP, 128), 0) == iota((CAP, 128), 1)

    def send_back(ws):
        ws = ws / math.sqrt(D)
        for k in range(LANES):
            row = jnp.sum(
                jnp.where(diagonal, ws[CAP * k : CAP * k + CAP], 0.0), axis=0, keepdims=True
            )
            ws_send[k] = jnp.broadcast_to(row, (8, 128))
        for c in range(4):
            halves = []
            for half in range(2):
                at = 1024 * half + 256 * c
                halves.append(
                    dot_nt(hb[0], wg[at : at + 256, :]) + dot_nt(hb[1], wu[at : at + 256, :])
                )
            both = []
            for k in range(LANES):
                both += [part[CAP * k : CAP * k + CAP] for part in halves]
            dx_send[:, 256 * c : 256 * c + 256] = jnp.concatenate(both, axis=0).astype(BF)

        def start(k):
            back_copy(k).start()
            value_copy(k).start()

        each_peer(start)
        dx_recv[pl.ds(pl.multiple_of(PAIR * me, 16), PAIR)] = dx_send[0:PAIR]
        ws_recv[me] = ws_send[0]

    def combine():
        def arrived(k):
            back_copy(k).wait_recv()
            value_copy(k).wait_recv()

        each_peer(arrived)
        for half, table in enumerate((place_l, place_r)):
            turned = table[...].astype(F32).T.astype(BF)
            for c in range(2):
                at = 1024 * half + 512 * c
                gx[:, at : at + 512] = dot(turned, dx_recv[:, 512 * c : 512 * c + 512]).astype(BF)
        chosen = []
        for s in range(LANES):
            column = jnp.sum(
                jnp.where(diagonal, ws_recv[s, 0:1, :], 0.0), axis=1, keepdims=True
            )
            one = place_l[PAIR * s : PAIR * s + PAIR].astype(F32)[0:CAP]
            chosen.append(jnp.sum(one * column, axis=0, keepdims=True))
        chosen = jnp.concatenate(chosen, axis=0)
        parts = [
            jnp.sum(jnp.where(ids_t[k : k + 1, :] == ex, chosen, 0.0), axis=0, keepdims=True)
            for k in range(8)
        ]
        values = (jnp.concatenate(parts, axis=0) / rw_t).astype(BF)
        gw[...] = dot_nt(eye(TOK), values).astype(BF)

        def left(k):
            back_copy(k).wait_send()
            value_copy(k).wait_send()

        each_peer(left)

    ws = hidden_chunk(0, jnp.zeros((ROWS, 1), F32))
    for j in range(3):
        product(j)
    ws = hidden_chunk(1, ws)
    ws = hidden_chunk(2, ws)
    send_back(ws)
    for g in range(3):
        now = range(3 * g, 3 * g + 3)
        last = range(3 * g - 3, 3 * g) if g else ()
        for j in now:
            x_step(j, 1)
        for j in last:
            z_step(j, 1)
        for j in now:
            x_step(j, 2)
        if g < 2:
            for j in now:
                product(j + 3)
        for j in last:
            z_step(j, 2)
        if g == 0:
            combine()
        for j in now:
            x_last(j)
        for j in last:
            z_last(j)
        if g:
            move_out(g - 1)
        if g > 1:
            move_in(g - 2)
        if g:
            move_pick(g - 1)
    for j in range(6, 9):
        z_step(j, 1)
    for j in range(6, 9):
        z_step(j, 2)
    for j in range(6, 9):
        z_last(j)
    move_out(2)
    move_in(1)
    each_peer(lambda k: dispatch(k).wait_send())
    move_pick(2)
    move_in(2)


def on_device(
    tokens, cotangent, route_ids, route_weights, capacity, old_owner, new_owner, w_gate, w_up, w_down
):
    vmem = pl.BlockSpec(memory_space=pltpu.VMEM)
    smem = pl.BlockSpec(memory_space=pltpu.SMEM)
    hbm = pl.BlockSpec(memory_space=pl.ANY)
    dma = pltpu.SemaphoreType.DMA
    shard = jax.ShapeDtypeStruct((1, 128, FFN), BF)
    V = pltpu.VMEM
    return pl.pallas_call(
        body,
        out_shape=(
            jax.ShapeDtypeStruct((TOK, D), BF),
            jax.ShapeDtypeStruct((TOK, 8), BF),
            shard, shard, shard,
        ),
        in_specs=[vmem] * 6 + [smem] * 2 + [hbm] * 3,
        out_specs=[vmem] * 5,
        scratch_shapes=[
            V((D, FFN), BF), V((D, FFN), BF), V((D, FFN), BF),
            V((2 * ROWS, D), BF), V((2 * ROWS, D), BF),
            V((ROWS, D), BF), V((ROWS, D), BF), V((3, ROWS, FFN), BF),
            V((UNITS, 4, 128, XBLK), BF), V((3, UNITS, 128, XBLK), BF),
            V((UNITS, 4, 128, ZBLK), BF), V((3, UNITS, 128, ZBLK), BF),
            V((2 * ROWS, D // 2), BF), V((2 * ROWS, D // 2), BF),
            V((LANES, 8, 128), F32), V((LANES, 8, 128), F32),
            V((2 * ROWS, TOK), BF), V((2 * ROWS, TOK), BF),
            V((3, 6, 128, 128), BF),
            V((LANES, 3, 16, 128), BF), V((LANES, 3, 16, 128), BF), V((LANES, 3, 16, 128), BF),
            V((3, LANES, 3, 16, 128), BF),
            V((3, 6, 128, 128), BF),
            pltpu.SMEM((LANES,), jnp.int32),
            dma((3,)),
            dma((LANES,)), dma((LANES,)),
            dma((3, UNITS)), dma((3, UNITS)),
            dma((3, UNITS)), dma((3, UNITS)),
            dma((LANES,)), dma((LANES,)), dma((LANES,)), dma((LANES,)),
            dma((3, LANES)), dma((3, LANES)), dma((3, LANES)), dma((3, LANES)),
        ],
        compiler_params=pltpu.CompilerParams(
            collective_id=0, has_side_effects=True, vmem_limit_bytes=62 * 1024 * 1024
        ),
        name="moe",
    )(
        tokens, cotangent, route_ids, route_weights,
        capacity[None], old_owner[None], old_owner, new_owner,
        w_gate, w_up, w_down,
    )


def solution(mesh):
    rows = P(("dp", "expert"), None)
    slots = P("expert", None, None)
    shards = P("expert", "dp", None)
    return jax.shard_map(
        on_device,
        mesh=mesh,
        in_specs=(rows, rows, rows, rows, P(), P(), P(), slots, slots, slots),
        out_specs=(rows, rows, shards, shards, shards),
        check_vma=False,
    )
```

```python
import math

import jax
import jax.numpy as jnp
from jax import lax
from jax.experimental import pallas as pl
from jax.experimental.pallas import tpu as pltpu
from jax.sharding import PartitionSpec as P

MESH = pl.DeviceIdType.MESH
CAP = 24
LANES = 16
TOK = 256
D = 2048
FFN = 768
ROWS = LANES * CAP
PAIR = 2 * CAP
COLS = 256
CHUNKS = FFN // COLS
UNITS = 6 * CHUNKS
PAIRS = UNITS // 2
AHEAD = 3
DIRECT = (7, 8)
GROUPS = ((0, 3), (3, 3), (6, 2), (8, 1))
XBLK = D // 4
ZBLK = XBLK // 4
BF = jnp.bfloat16
F32 = jnp.float32
NT = (((1,), (1,)), ((), ()))


def iota(shape, dim):
    return lax.broadcasted_iota(jnp.int32, shape, dim)


def dot(a, b):
    return jnp.dot(a, b, preferred_element_type=F32)


def dot_nt(a, b):
    return lax.dot_general(a, b, NT, preferred_element_type=F32)


PLAN = (
    (),
    (("product", 0),),
    (("product", 1),),
    (("product", 2),),
    (("product", 3), ("step", 0, 1), ("step", 1, 1), ("step", 2, 1), ("combine",)),
    (("product", 4), ("step", 0, 2), ("step", 1, 2), ("step", 2, 2), ("step", 3, 1)),
    (("product", 5), ("last", 0), ("last", 1), ("last", 2), ("out", 0), ("step", 3, 2), ("step", 4, 1)),
    (("product", 6), ("last", 3), ("step", 4, 2), ("step", 5, 1)),
    (("product", 7), ("last", 4), ("step", 5, 2), ("step", 6, 1), ("pick", 0)),
    (("last", 5), ("out", 1), ("product", 8), ("step", 6, 2), ("last", 7), ("in", 0)),
    (("last", 6), ("out", 2), ("last", 8), ("out", 3)),
)


NEAR = (1, 2, 3, 4, 12, 5, 13, 6, 14, 7, 15, 8, 9, 10, 11)


def body(
    tok_h, cot_h, ids, rw, cap, old, old_s, new_s, wg_h, wu_h, wd_h,
    gx_h, gw, gg_h, gu_h, gd_h,
    tok, cot, wg, wu, wd, xs_send, xs_recv, xf, xb, sb, x4, s4, hb, ht, zb, zr,
    dx_send, dx_recv, ws_send, ws_recv, place_l, place_r, gx, gbuf, p1a, p1b, p1c, p1d, p2a, p2b, p2c, p2d, ob, go, wanted,
    w_sem, t_sem, o_sem, d_ss, d_rs, f_ss, f_rs, a_ss, a_rs, g_ss, g_rs, z_ss, z_rs,
    b_ss, b_rs, v_ss, v_rs, p_ss, p_rs, q_ss, q_rs,
):
    dp = lax.axis_index("dp")
    me = lax.axis_index("expert")
    x, zh = dp // 4, dp % 4
    y, zl, co = me // 4, (me // 2) % 2, me % 2
    p1, p2 = (p1a, p1b, p1c, p1d), (p2a, p2b, p2c, p2d)

    def at_x(s):
        return (((x + s + 4) % 4) * 4 + zh, me)

    def at_z(s):
        return (x * 4 + (zh + s + 4) % 4, me)

    def ahead(k):
        return ((y + k // 4) % 4) * 4 + ((zl + (k // 2) % 2) % 2) * 2 + (co + k % 2) % 2

    def behind(k):
        return ((y + 4 - k // 4) % 4) * 4 + ((zl + (k // 2) % 2) % 2) * 2 + (co + k % 2) % 2

    def remote(src, dst, ss, rs, device):
        return pltpu.make_async_remote_copy(
            src_ref=src, dst_ref=dst, send_sem=ss, recv_sem=rs,
            device_id=device, device_id_type=MESH,
        )

    def drain(ref, sem):
        pltpu.make_async_copy(ref, ref, sem).wait()

    rows_in = [
        pltpu.make_async_copy(h, v, t_sem.at[i])
        for i, (h, v) in enumerate(((tok_h, tok), (cot_h, cot)))
    ]
    weights = [
        pltpu.make_async_copy(h.at[0], v, w_sem.at[i])
        for i, (h, v) in enumerate(((wg_h, wg), (wu_h, wu), (wd_h, wd)))
    ]
    for copy in rows_in + weights:
        copy.start()
    barrier = pltpu.get_barrier_semaphore()
    for k in NEAR:
        pl.semaphore_signal(barrier, inc=1, device_id=(dp, ahead(k)), device_id_type=MESH)
    for s in (1, 2, 3):
        pl.semaphore_signal(barrier, inc=1, device_id=at_x(s), device_id_type=MESH)
    for s in (1, 2, 3):
        pl.semaphore_signal(barrier, inc=1, device_id=at_z(s), device_id_type=MESH)

    ids_t = ids[...].astype(F32)
    rw_t = rw[...].astype(F32)
    mine = old[...] == iota((LANES, LANES), 0)
    ex = jnp.sum(jnp.where(mine, iota((LANES, LANES), 1), 0).astype(F32), axis=1, keepdims=True)
    limit = jnp.sum(jnp.where(mine, cap[...], 0).astype(F32), axis=1, keepdims=True)
    named = jnp.zeros((LANES, TOK), F32)
    w_sel = jnp.zeros((LANES, TOK), F32)
    for k in range(8):
        hit = ids_t[k : k + 1, :] == ex
        named = named + jnp.where(hit, 1.0, 0.0)
        w_sel = w_sel + jnp.where(hit, rw_t[k : k + 1, :], 0.0)
    earlier = (iota((TOK, TOK), 0) < iota((TOK, TOK), 1)).astype(F32).astype(BF)
    before = dot(named.astype(BF), earlier)
    pos = jnp.where((named > 0.5) & (before < limit), before, -1.0)
    p_of = iota((CAP, TOK), 0).astype(F32)
    ones = [jnp.where(pos[s : s + 1, :] == p_of, 1.0, 0.0) for s in range(LANES)]
    place = jnp.concatenate(ones, axis=0).astype(BF)
    place_w = jnp.concatenate(
        [one * w_sel[s : s + 1, :] for s, one in enumerate(ones)], axis=0
    ).astype(BF)
    for copy in rows_in:
        copy.wait()
    for c in range(D // 256):
        cols = slice(256 * c, 256 * c + 256)
        rows_x = dot(place, tok[:, cols])
        rows_s = dot(place_w, cot[:, cols])
        both = []
        for s in range(LANES):
            both += [rows_x[CAP * s : CAP * s + CAP], rows_s[CAP * s : CAP * s + CAP]]
        xs_send[:, cols] = jnp.concatenate(both, axis=0).astype(BF)

    pl.semaphore_wait(barrier, LANES - 1 + 6)

    def block(k):
        return pl.ds(PAIR * k, PAIR)

    def dispatch(k):
        to = ahead(k)
        return remote(
            xs_send.at[pl.ds(pl.multiple_of(PAIR * to, 16), PAIR)], xs_recv.at[block(k)],
            d_ss, d_rs.at[k], (dp, to),
        )

    def columns(s):
        return pl.ds(pl.multiple_of(XBLK * ((x + s) % 4), XBLK), XBLK)

    def forward(k):
        for s in (2, 1, 3):
            remote(
                xs_recv.at[block(k), columns(s)], xf.at[s - 1, block(k)],
                f_ss, f_rs.at[s - 1], at_x(s),
            ).start()

    for k in NEAR:
        dispatch(k).start()
    xs_recv[0:PAIR] = xs_send[pl.ds(pl.multiple_of(PAIR * me, 16), PAIR)]
    forward(0)

    nothing = jnp.zeros((CAP, TOK), F32)
    left, right = [], []
    for one in ones:
        left += [one, nothing]
        right += [nothing, one]
    place_l[...] = jnp.concatenate(left, axis=0).astype(BF)
    place_r[...] = jnp.concatenate(right, axis=0).astype(BF)

    def look_up(j, carry):
        slot = jnp.int32(0)
        for n in range(LANES):
            slot = slot + jnp.where(new_s[n] == j, old_s[n], 0)
        wanted[j] = slot
        return carry

    lax.fori_loop(0, LANES, look_up, 0)
    for copy in weights:
        copy.wait()
    for k in NEAR:
        dispatch(k).wait_recv()
        forward(k)

    def split(src, cols):
        both = src[:, cols].astype(F32)
        return [
            jnp.concatenate(
                [both[PAIR * k + at : PAIR * k + at + CAP] for k in range(LANES)], axis=0
            ).astype(BF)
            for at in (0, CAP)
        ]

    for c in range(D // 256):
        cols = slice(256 * c, 256 * c + 256)
        xb[:, cols], sb[:, cols] = split(xs_recv, cols)

    def hidden_chunk(c, ws):
        cols = slice(COLS * c, COLS * c + COLS)
        gate = dot(xb[...], wg[:, cols])
        up = dot(xb[...], wu[:, cols])
        dh = dot(sb[...], wd[:, cols])
        sig = 1.0 / (1.0 + jnp.exp(-gate))
        act = gate * sig
        hidden = (act * up).astype(BF)
        dgate = dh * up * (sig * (1.0 + gate * (1.0 - sig)))
        dup = dh * act
        hb[0, :, cols] = dgate.astype(BF)
        hb[1, :, cols] = dup.astype(BF)
        hidden = hidden.astype(F32)
        for m, value in enumerate((dgate, dup, hidden)):
            turned = value.T.astype(BF)
            for h in range(2):
                ht[0, 6 * c + 2 * m + h] = turned[128 * h : 128 * h + 128]
        return ws + jnp.sum(hidden * dh, axis=1, keepdims=True)

    scale = 1.0 / math.sqrt(4 * 4 * LANES * CAP)

    def units_of(j):
        return (2 * j, 2 * j + 1)

    def sign(u):
        return 1 if u % 2 == 0 else -1

    def share(u, s):
        slot = 1 if s == 1 else 3
        return remote(ht.at[0, u], ht.at[slot, u], a_ss.at[slot // 2, u], a_rs.at[slot // 2, u], at_x(s))

    def pass_on(u):
        s = sign(u)
        return remote(ht.at[1 if s == 1 else 3, u], ht.at[2, u], g_ss.at[u], g_rs.at[u], at_x(s))

    def share_start(j):
        up, down = units_of(j)
        share(up, 1).start()
        share(down, -1).start()
        share(down, 1).start()
        share(up, -1).start()

    def share_pass(j):
        for u in units_of(j):
            share(u, sign(u)).wait_recv()
            pass_on(u).start()

    def share_rest(j):
        for u in units_of(j):
            share(u, -sign(u)).wait_recv()

    def z_block(u, k):
        return (zh - sign(u) * (1 + k) + 8) % 4

    def z_copy(u, k):
        return remote(
            zb.at[u, z_block(u, k)], zr.at[k, u], z_ss.at[k, u], z_rs.at[k, u], at_z(sign(u))
        )

    def z_direct(j, s):
        both = pl.ds(2 * j, 2)
        return remote(
            zb.at[both, (zh + s) % 4], zr.at[s - 1, both],
            z_ss.at[s - 1, 2 * j], z_rs.at[s - 1, 2 * j], at_z(s),
        )

    def product(j):
        rows = s4 if j % 3 == 2 else x4
        up, down = units_of(j)
        total = jnp.zeros((COLS, XBLK), F32)
        for s in (0, 1, 3, 2):
            if s == 2:
                for u in units_of(j):
                    pass_on(u).wait_recv()
            total = total + dot(ht[s, up : down + 1].reshape(COLS, ROWS), rows[s])
        total = (total * scale).astype(BF)
        for h, u in enumerate(units_of(j)):
            for q in range(4):
                zb[u, q] = total[128 * h : 128 * h + 128, ZBLK * q : ZBLK * q + ZBLK]
            if j not in DIRECT:
                z_copy(u, 0).start()
        if j in DIRECT:
            for s in (2, 1, 3):
                z_direct(j, s).start()
        for u in units_of(j):
            share(u, 1).wait_send()
            share(u, -1).wait_send()
            pass_on(u).wait_send()

    def z_step(j, k):
        for u in units_of(j):
            z_copy(u, k - 1).wait_recv()
            b = z_block(u, k)
            zb[u, b] = (zb[u, b].astype(F32) + zr[k - 1, u].astype(F32)).astype(BF)
            z_copy(u, k).start()
            z_copy(u, k - 1).wait_send()

    def z_last(j):
        if j in DIRECT:
            for s in (1, 3, 2):
                z_direct(j, s).wait_recv()
            for u in units_of(j):
                total = zb[u, zh].astype(F32)
                for s in range(3):
                    total = total + zr[s, u].astype(F32)
                gbuf[u] = total.T.astype(BF)
            for s in (1, 3, 2):
                z_direct(j, s).wait_send()
            return
        for u in units_of(j):
            z_copy(u, 2).wait_recv()
            total = zb[u, zh].astype(F32) + zr[2, u].astype(F32)
            gbuf[u] = total.T.astype(BF)
            z_copy(u, 2).wait_send()

    def piece(g, n):
        first, count = GROUPS[g]
        units = pl.ds(2 * first + count * (n % 2), count)
        return units, pl.ds(pl.multiple_of(16 * (n // 2), 16), 16)

    def move_out(g):
        for k in NEAR:
            to = ahead(k)
            remote(
                gbuf.at[*piece(g, to)], p1[g].at[me], p_ss.at[g], p_rs.at[g], (dp, to)
            ).start()
        p1[g][me] = gbuf[*piece(g, me)]

    def move_pick(g):
        drain(p1[g].at[0 : LANES - 1], p_rs.at[g])

        def pick(j, carry):
            p2[g][j] = p1[g][wanted[j]]
            return carry

        lax.fori_loop(0, LANES, pick, 0)
        for k in NEAR:
            to = ahead(k)
            remote(
                p2[g].at[to], ob.at[*piece(g, me)], q_ss.at[g], q_rs.at[g], (dp, to)
            ).start()
        ob[*piece(g, me)] = p2[g][me]
        drain(p1[g].at[0 : LANES - 1], p_ss.at[g])

    def result(j):
        cols = pl.ds(COLS * (j // 3), COLS)
        return pltpu.make_async_copy(
            go.at[j % 3, :, cols], (gg_h, gu_h, gd_h)[j % 3].at[0, :, cols], o_sem.at[1 + j]
        )

    def move_in(g):
        drain(p2[g].at[0 : LANES - 1], q_rs.at[g])
        first, count = GROUPS[g]
        for j in range(first, first + count):
            for h, u in enumerate(units_of(j)):
                at = COLS * (j // 3) + 128 * h
                go[j % 3, :, at : at + 128] = ob[u]
            result(j).start()
        drain(p2[g].at[0 : LANES - 1], q_ss.at[g])

    diagonal = iota((CAP, 128), 0) == iota((CAP, 128), 1)

    def send_back(ws):
        ws = ws / math.sqrt(D)
        for k in range(LANES):
            row = jnp.sum(
                jnp.where(diagonal, ws[CAP * k : CAP * k + CAP], 0.0), axis=0, keepdims=True
            )
            ws_send[k] = jnp.broadcast_to(row, (8, 128))
        for c in range(4):
            halves = []
            for half in range(2):
                at = 1024 * half + 256 * c
                halves.append(
                    dot_nt(hb[0], wg[at : at + 256, :]) + dot_nt(hb[1], wu[at : at + 256, :])
                )
            both = []
            for k in range(LANES):
                both += [part[CAP * k : CAP * k + CAP] for part in halves]
            dx_send[:, 256 * c : 256 * c + 256] = jnp.concatenate(both, axis=0).astype(BF)
        at_me = pl.ds(pl.multiple_of(PAIR * me, 16), PAIR)
        for k in NEAR:
            to = behind(k)
            remote(dx_send.at[block(k)], dx_recv.at[at_me], b_ss, b_rs, (dp, to)).start()
            remote(ws_send.at[k], ws_recv.at[me], v_ss, v_rs, (dp, to)).start()
        dx_recv[at_me] = dx_send[0:PAIR]
        ws_recv[me] = ws_send[0]

    gx_out = pltpu.make_async_copy(gx, gx_h, o_sem.at[0])

    def combine():
        drain(dx_send.at[0 : PAIR * (LANES - 1)], b_rs)
        drain(ws_send.at[0 : LANES - 1], v_rs)
        for half, table in enumerate((place_l, place_r)):
            turned = table[...].astype(F32).T.astype(BF)
            for c in range(2):
                at = 1024 * half + 512 * c
                gx[:, at : at + 512] = dot(turned, dx_recv[:, 512 * c : 512 * c + 512]).astype(BF)
        gx_out.start()
        chosen = []
        for s in range(LANES):
            column = jnp.sum(
                jnp.where(diagonal, ws_recv[s, 0:1, :], 0.0), axis=1, keepdims=True
            )
            one = place_l[PAIR * s : PAIR * s + PAIR].astype(F32)[0:CAP]
            chosen.append(jnp.sum(one * column, axis=0, keepdims=True))
        chosen = jnp.concatenate(chosen, axis=0)
        parts = [
            jnp.sum(jnp.where(ids_t[k : k + 1, :] == ex, chosen, 0.0), axis=0, keepdims=True)
            for k in range(8)
        ]
        gw[...] = (jnp.concatenate(parts, axis=0) / rw_t).astype(BF)
        drain(dx_send.at[0 : PAIR * (LANES - 1)], b_ss)
        drain(ws_send.at[0 : LANES - 1], v_ss)

    ws = hidden_chunk(0, jnp.zeros((ROWS, 1), F32))
    for j in range(AHEAD):
        share_start(j)
    ws = hidden_chunk(1, ws)
    ws = hidden_chunk(2, ws)
    send_back(ws)
    for s in range(4):
        if s == 0:
            own = pl.ds(pl.multiple_of(XBLK * x, XBLK), XBLK)
            x4[0], s4[0] = xb[:, own], sb[:, own]
        else:
            drain(xf.at[s - 1], f_rs.at[s - 1])
            x4[s], s4[s] = split(xf.at[s - 1], slice(None))
    drain(xs_send.at[0 : PAIR * (LANES - 1)], d_ss)
    drain(xf, f_ss)
    for j in range(PAIRS + 2):
        if j < PAIRS:
            share_pass(j)
        if j + AHEAD < PAIRS:
            share_start(j + AHEAD)
        if j < PAIRS:
            share_rest(j)
        for step, *args in PLAN[j]:
            {
                "product": product, "step": z_step, "last": z_last, "combine": combine,
                "out": move_out, "pick": move_pick, "in": move_in,
            }[step](*args)
    for g in range(1, 4):
        move_pick(g)
    for g in range(1, 4):
        move_in(g)
    gx_out.wait()
    for j in range(PAIRS):
        result(j).wait()


def hand_over(*refs):
    sources, results, held, sems = refs[:5], refs[5:10], refs[10:15], refs[15]
    arrive = [
        pltpu.make_async_copy(a, b, sems.at[0, i]) for i, (a, b) in enumerate(zip(sources, held))
    ]
    leave = [
        pltpu.make_async_copy(a, b, sems.at[1, i]) for i, (a, b) in enumerate(zip(held, results))
    ]
    for copy in arrive:
        copy.start()
    for before, after in zip(arrive, leave):
        before.wait()
        after.start()
    for copy in leave:
        copy.wait()


def on_device(
    tokens, cotangent, route_ids, route_weights, capacity, old_owner, new_owner, w_gate, w_up, w_down
):
    vmem = pl.BlockSpec(memory_space=pltpu.VMEM)
    smem = pl.BlockSpec(memory_space=pltpu.SMEM)
    hbm = pl.BlockSpec(memory_space=pl.ANY)
    dma = pltpu.SemaphoreType.DMA
    shard = jax.ShapeDtypeStruct((1, 128, FFN), BF)
    shapes = (
        jax.ShapeDtypeStruct((TOK, D), BF),
        jax.ShapeDtypeStruct((8, TOK), BF),
        shard, shard, shard,
    )
    V = pltpu.VMEM
    parts = pl.pallas_call(
        body,
        out_shape=shapes,
        in_specs=[hbm] * 2 + [vmem] * 4 + [smem] * 2 + [hbm] * 3,
        out_specs=[hbm, vmem, hbm, hbm, hbm],
        scratch_shapes=[
            V((TOK, D), BF), V((TOK, D), BF),
            V((D, FFN), BF), V((D, FFN), BF), V((D, FFN), BF),
            V((2 * ROWS, D), BF), V((2 * ROWS, D), BF), V((3, 2 * ROWS, XBLK), BF),
            V((ROWS, D), BF), V((ROWS, D), BF),
            V((4, ROWS, XBLK), BF), V((4, ROWS, XBLK), BF),
            V((2, ROWS, FFN), BF), V((4, UNITS, 128, ROWS), BF),
            V((UNITS, 4, 128, ZBLK), BF), V((3, UNITS, 128, ZBLK), BF),
            V((2 * ROWS, D // 2), BF), V((2 * ROWS, D // 2), BF),
            V((LANES, 8, 128), F32), V((LANES, 8, 128), F32),
            V((2 * ROWS, TOK), BF), V((2 * ROWS, TOK), BF),
            V((TOK, D), BF),
            V((UNITS, 128, 128), BF),
            *[V((LANES, count, 16, 128), BF) for _, count in GROUPS + GROUPS],
            V((UNITS, 128, 128), BF),
            V((3, 128, FFN), BF),
            pltpu.SMEM((LANES,), jnp.int32),
            dma((3,)), dma((2,)), dma((1 + PAIRS,)),
            dma, dma((LANES,)), dma, dma((3,)),
            dma((2, UNITS)), dma((2, UNITS)), dma((UNITS,)), dma((UNITS,)),
            dma((3, UNITS)), dma((3, UNITS)),
            dma, dma, dma, dma,
            dma((4,)), dma((4,)), dma((4,)), dma((4,)),
        ],
        compiler_params=pltpu.CompilerParams(
            collective_id=0, has_side_effects=True, vmem_limit_bytes=62 * 1024 * 1024
        ),
        name="moe",
    )(
        tokens, cotangent, route_ids.T, route_weights.T,
        capacity[None], old_owner[None], old_owner, new_owner,
        w_gate, w_up, w_down,
    )
    grad_x, grad_w, gate, up, down = pl.pallas_call(
        hand_over,
        out_shape=shapes,
        in_specs=[hbm] * 5,
        out_specs=[hbm] * 5,
        scratch_shapes=[V(held.shape, BF) for held in shapes] + [dma((2, 5))],
        compiler_params=pltpu.CompilerParams(vmem_limit_bytes=62 * 1024 * 1024),
        name="results",
    )(*parts)
    return grad_x, grad_w.T, gate, up, down


def solution(mesh):
    rows = P(("dp", "expert"), None)
    slots = P("expert", None, None)
    shards = P("expert", "dp", None)
    return jax.shard_map(
        on_device,
        mesh=mesh,
        in_specs=(rows, rows, rows, rows, P(), P(), P(), slots, slots, slots),
        out_specs=(rows, rows, shards, shards, shards),
        check_vma=False,
    )
```

```python
import math

import jax
import jax.numpy as jnp
from jax import lax
from jax.experimental import pallas as pl
from jax.experimental.pallas import tpu as pltpu
from jax.sharding import PartitionSpec as P

MESH = pl.DeviceIdType.MESH
CAP = 24
LANES = 16
TOK = 256
D = 2048
FFN = 768
ROWS = LANES * CAP
PAIR = 2 * CAP
COLS = 256
CHUNKS = FFN // COLS
UNITS = 6 * CHUNKS
PAIRS = UNITS // 2
AHEAD = 3
GROUPS = ((0, 4), (4, 3), (7, 2))
XBLK = D // 4
ZBLK = XBLK // 4
BF = jnp.bfloat16
F32 = jnp.float32
NT = (((1,), (1,)), ((), ()))


def iota(shape, dim):
    return lax.broadcasted_iota(jnp.int32, shape, dim)


def dot(a, b):
    return jnp.dot(a, b, preferred_element_type=F32)


def dot_nt(a, b):
    return lax.dot_general(a, b, NT, preferred_element_type=F32)


PLAN = (
    (),
    (("product", 0),),
    (("product", 1),),
    (("product", 2), ("last", 0), ("combine",)),
    (("product", 3), ("last", 1)),
    (("product", 4), ("last", 2)),
    (("product", 5), ("last", 3), ("out", 0)),
    (("product", 6), ("last", 4), ("pick", 0)),
    (("product", 7), ("product", 8), ("last", 5), ("in", 0)),
    (
        ("last", 6), ("out", 1), ("last", 7), ("last", 8), ("out", 2),
        ("pick", 1), ("pick", 2), ("in", 1), ("in", 2),
    ),
)


NEAR = (1, 2, 3, 4, 12, 5, 13, 6, 14, 7, 15, 8, 9, 10, 11)
HALF = ROWS // 2


def body(
    tok_h, cot_h, ids, rw, cap, old, old_s, new_s, wg_h, wu_h, wd_h,
    gx_h, gw, gg_h, gu_h, gd_h,
    tok, cot, wg, wu, wd, xs_send, xs_recv, xf, xb, sb, x4, s4, hb, ht, zb, zr,
    dx_send, dx_recv, ws_send, ws_recv, place_l, place_r, gx, gbuf, ob, go, wanted,
    w_sem, t_sem, o_sem, d_ss, d_rs, f_ss, f_rs, a_ss, a_rs, g_ss, g_rs, z_ss, z_rs,
    b_ss, b_rs, v_ss, v_rs, p_ss, p_rs, q_ss, q_rs, *moved,
):
    dp = lax.axis_index("dp")
    me = lax.axis_index("expert")
    x, zh = lax.div(dp, 4), lax.rem(dp, 4)
    y, zl, co = lax.div(me, 4), lax.rem(lax.div(me, 2), 2), lax.rem(me, 2)
    p1, p2 = moved[: len(GROUPS)], moved[len(GROUPS) :]

    def at_x(s):
        return (lax.rem(x + (s + 4) % 4, 4) * 4 + zh, me)

    def at_z(s):
        return (x * 4 + lax.rem(zh + (s + 4) % 4, 4), me)

    def ahead(k):
        return lax.rem(y + k // 4, 4) * 4 + lax.rem(zl + (k // 2) % 2, 2) * 2 + lax.rem(co + k % 2, 2)

    def behind(k):
        return lax.rem(y + 4 - k // 4, 4) * 4 + lax.rem(zl + (k // 2) % 2, 2) * 2 + lax.rem(co + k % 2, 2)

    def remote(src, dst, ss, rs, device):
        return pltpu.make_async_remote_copy(
            src_ref=src, dst_ref=dst, send_sem=ss, recv_sem=rs,
            device_id=device, device_id_type=MESH,
        )

    def drain(ref, sem):
        pltpu.make_async_copy(ref, ref, sem).wait()

    rows_in = [
        pltpu.make_async_copy(h, v, t_sem.at[i])
        for i, (h, v) in enumerate(((tok_h, tok), (cot_h, cot)))
    ]
    weights = [
        pltpu.make_async_copy(h.at[0], v, w_sem.at[i])
        for i, (h, v) in enumerate(((wg_h, wg), (wu_h, wu), (wd_h, wd)))
    ]
    for copy in rows_in + weights:
        copy.start()
    barrier = pltpu.get_barrier_semaphore()
    for k in NEAR:
        pl.semaphore_signal(barrier, inc=1, device_id=(dp, ahead(k)), device_id_type=MESH)
    for s in (1, 2, 3):
        pl.semaphore_signal(barrier, inc=1, device_id=at_x(s), device_id_type=MESH)
    for s in (1, 2, 3):
        pl.semaphore_signal(barrier, inc=1, device_id=at_z(s), device_id_type=MESH)

    ids_t = ids[...].astype(F32)
    rw_t = rw[...].astype(F32)
    mine = old[...] == iota((LANES, LANES), 0)
    ex = jnp.sum(jnp.where(mine, iota((LANES, LANES), 1), 0).astype(F32), axis=1, keepdims=True)
    limit = jnp.sum(jnp.where(mine, cap[...], 0).astype(F32), axis=1, keepdims=True)
    named = jnp.zeros((LANES, TOK), F32)
    w_sel = jnp.zeros((LANES, TOK), F32)
    for k in range(8):
        hit = ids_t[k : k + 1, :] == ex
        named = named + jnp.where(hit, 1.0, 0.0)
        w_sel = w_sel + jnp.where(hit, rw_t[k : k + 1, :], 0.0)
    earlier = (iota((TOK, TOK), 0) < iota((TOK, TOK), 1)).astype(F32).astype(BF)
    before = dot(named.astype(BF), earlier)
    pos = jnp.where((named > 0.5) & (before < limit), before, -1.0)
    p_of = iota((CAP, TOK), 0).astype(F32)
    ones = [jnp.where(pos[s : s + 1, :] == p_of, 1.0, 0.0) for s in range(LANES)]
    place = jnp.concatenate(ones, axis=0).astype(BF)
    place_w = jnp.concatenate(
        [one * w_sel[s : s + 1, :] for s, one in enumerate(ones)], axis=0
    ).astype(BF)
    for copy in rows_in:
        copy.wait()
    for c in range(D // 256):
        cols = slice(256 * c, 256 * c + 256)
        rows_x = dot(place, tok[:, cols])
        rows_s = dot(place_w, cot[:, cols])
        both = []
        for s in range(LANES):
            both += [rows_x[CAP * s : CAP * s + CAP], rows_s[CAP * s : CAP * s + CAP]]
        xs_send[:, cols] = jnp.concatenate(both, axis=0).astype(BF)

    pl.semaphore_wait(barrier, LANES - 1 + 6)

    def place_of(k):
        return ((0,) + NEAR).index(k)

    def block(k):
        return pl.ds(PAIR * place_of(k), PAIR)

    def dispatch(k):
        to = ahead(k)
        return remote(
            xs_send.at[pl.ds(pl.multiple_of(PAIR * to, 16), PAIR)], xs_recv.at[block(k)],
            d_ss, d_rs.at[k], (dp, to),
        )

    def columns(s):
        return pl.ds(pl.multiple_of(XBLK * lax.rem(x + s, 4), XBLK), XBLK)

    def forward(k):
        for s in (2, 1, 3):
            remote(
                xs_recv.at[block(k), columns(s)], xf.at[s - 1, block(k)],
                f_ss, f_rs.at[s - 1], at_x(s),
            ).start()

    for k in NEAR:
        dispatch(k).start()
    xs_recv[0:PAIR] = xs_send[pl.ds(pl.multiple_of(PAIR * me, 16), PAIR)]
    forward(0)

    nothing = jnp.zeros((CAP, TOK), F32)
    left, right = [], []
    for one in ones:
        left += [one, nothing]
        right += [nothing, one]
    place_l[...] = jnp.concatenate(left, axis=0).astype(BF)
    place_r[...] = jnp.concatenate(right, axis=0).astype(BF)

    def look_up(j, carry):
        slot = jnp.int32(0)
        for n in range(LANES):
            slot = slot + jnp.where(new_s[n] == j, old_s[n], 0)
        wanted[j] = slot
        return carry

    lax.fori_loop(0, LANES, look_up, 0)
    for copy in weights:
        copy.wait()
    def split(src, cols, first=0, count=LANES):
        both = src[PAIR * first : PAIR * (first + count), cols].astype(F32)
        return [
            jnp.concatenate(
                [both[PAIR * k + at : PAIR * k + at + CAP] for k in range(count)], axis=0
            ).astype(BF)
            for at in (0, CAP)
        ]

    def unpack(half):
        rows = slice(HALF * half, HALF * half + HALF)
        for c in range(D // 256):
            cols = slice(256 * c, 256 * c + 256)
            xb[rows, cols], sb[rows, cols] = split(xs_recv, cols, LANES // 2 * half, LANES // 2)

    def hidden_chunk(half, c):
        rows = slice(HALF * half, HALF * half + HALF)
        cols = slice(COLS * c, COLS * c + COLS)
        gate = dot(xb[rows], wg[:, cols])
        up = dot(xb[rows], wu[:, cols])
        dh = dot(sb[rows], wd[:, cols])
        sig = 1.0 / (1.0 + jnp.exp(-gate))
        act = gate * sig
        hidden = (act * up).astype(BF)
        hb[0, rows, cols] = (dh * up * (sig * (1.0 + gate * (1.0 - sig)))).astype(BF)
        hb[1, rows, cols] = (dh * act).astype(BF)
        hb[2, rows, cols] = hidden
        return jnp.sum(hidden.astype(F32) * dh, axis=1, keepdims=True)

    def turn(c):
        for m in range(3):
            turned = hb[m, :, COLS * c : COLS * c + COLS].astype(F32).T.astype(BF)
            for h in range(2):
                ht[0, 6 * c + 2 * m + h] = turned[128 * h : 128 * h + 128]

    scale = 1.0 / math.sqrt(4 * 4 * LANES * CAP)

    def units_of(j):
        return (2 * j, 2 * j + 1)

    def sign(u):
        return 1 if u % 2 == 0 else -1

    def share(u, s):
        slot = 1 if s == 1 else 3
        return remote(ht.at[0, u], ht.at[slot, u], a_ss.at[slot // 2, u], a_rs.at[slot // 2, u], at_x(s))

    def pass_on(u):
        s = sign(u)
        return remote(ht.at[1 if s == 1 else 3, u], ht.at[2, u], g_ss.at[u], g_rs.at[u], at_x(s))

    def share_start(j):
        up, down = units_of(j)
        share(up, 1).start()
        share(down, -1).start()
        share(down, 1).start()
        share(up, -1).start()

    def share_pass(j):
        for u in units_of(j):
            share(u, sign(u)).wait_recv()
            pass_on(u).start()

    def share_rest(j):
        for u in units_of(j):
            share(u, -sign(u)).wait_recv()

    def z_copy(j, s):
        both = pl.ds(2 * j, 2)
        return remote(
            zb.at[both, lax.rem(zh + s, 4)], zr.at[s - 1, both],
            z_ss.at[s - 1, j], z_rs.at[s - 1, j], at_z(s),
        )

    def product(j):
        rows = s4 if j % 3 == 2 else x4
        up, down = units_of(j)
        total = jnp.zeros((COLS, XBLK), F32)
        for s in (0, 1, 3, 2):
            if s == 2:
                for u in units_of(j):
                    pass_on(u).wait_recv()
            total = total + dot(ht[s, up : down + 1].reshape(COLS, ROWS), rows[s])
        total = (total * scale).astype(BF)
        for h, u in enumerate(units_of(j)):
            for q in range(4):
                zb[u, q] = total[128 * h : 128 * h + 128, ZBLK * q : ZBLK * q + ZBLK]
        for s in (2, 1, 3):
            z_copy(j, s).start()
        for u in units_of(j):
            share(u, 1).wait_send()
            share(u, -1).wait_send()
            pass_on(u).wait_send()

    def z_last(j):
        for s in (1, 3, 2):
            z_copy(j, s).wait_recv()
        for u in units_of(j):
            total = zb[u, zh].astype(F32)
            for s in range(3):
                total = total + zr[s, u].astype(F32)
            gbuf[u] = total.T.astype(BF)
        for s in (1, 3, 2):
            z_copy(j, s).wait_send()

    def piece(g, n):
        first, count = GROUPS[g]
        units = pl.ds(2 * first + count * lax.rem(n, 2), count)
        return units, pl.ds(pl.multiple_of(16 * lax.div(n, 2), 16), 16)

    def move_out(g):
        first, count = GROUPS[g]
        for n in range(LANES):

            @pl.when(n != me)
            def _(n=n):
                at = 2 * first + count * (n % 2)
                part = gbuf.at[at : at + count, 16 * (n // 2) : 16 * (n // 2) + 16]
                remote(part, p1[g].at[me], p_ss.at[g], p_rs.at[g], (dp, n)).start()
        p1[g][me] = gbuf[*piece(g, me)]

    def move_pick(g):
        drain(p1[g].at[0 : LANES - 1], p_rs.at[g])

        def pick(j, carry):
            p2[g][j] = p1[g][wanted[j]]
            return carry

        lax.fori_loop(0, LANES, pick, 0)
        here = ob.at[*piece(g, me)]
        for n in range(LANES):

            @pl.when(n != me)
            def _(n=n):
                remote(p2[g].at[n], here, q_ss.at[g], q_rs.at[g], (dp, n)).start()
        ob[*piece(g, me)] = p2[g][me]
        drain(p1[g].at[0 : LANES - 1], p_ss.at[g])

    def result(j):
        cols = pl.ds(COLS * (j // 3), COLS)
        return pltpu.make_async_copy(
            go.at[j % 3, :, cols], (gg_h, gu_h, gd_h)[j % 3].at[0, :, cols], o_sem.at[1 + j]
        )

    def move_in(g):
        drain(p2[g].at[0 : LANES - 1], q_rs.at[g])
        first, count = GROUPS[g]
        for j in range(first, first + count):
            for h, u in enumerate(units_of(j)):
                at = COLS * (j // 3) + 128 * h
                go[j % 3, :, at : at + 128] = ob[u]
            result(j).start()
        drain(p2[g].at[0 : LANES - 1], q_ss.at[g])

    diagonal = iota((CAP, 128), 0) == iota((CAP, 128), 1)

    def back_rows(half, ws):
        ws = ws / math.sqrt(D)
        rows = slice(HALF * half, HALF * half + HALF)
        for k in range(LANES // 2):
            row = jnp.sum(
                jnp.where(diagonal, ws[CAP * k : CAP * k + CAP], 0.0), axis=0, keepdims=True
            )
            ws_send[LANES // 2 * half + k] = jnp.broadcast_to(row, (8, 128))
        for c in range(4):
            sides = []
            for side in range(2):
                at = 1024 * side + 256 * c
                sides.append(
                    dot_nt(hb[0, rows], wg[at : at + 256, :])
                    + dot_nt(hb[1, rows], wu[at : at + 256, :])
                )
            both = []
            for k in range(LANES // 2):
                both += [part[CAP * k : CAP * k + CAP] for part in sides]
            dx_send[2 * HALF * half : 2 * HALF * (half + 1), 256 * c : 256 * c + 256] = (
                jnp.concatenate(both, axis=0).astype(BF)
            )

    def back_start(half):
        at_me = pl.ds(pl.multiple_of(PAIR * me, 16), PAIR)
        for k in NEAR:
            if place_of(k) // (LANES // 2) != half:
                continue
            to = behind(k)
            remote(dx_send.at[block(k)], dx_recv.at[at_me], b_ss, b_rs, (dp, to)).start()
            remote(ws_send.at[place_of(k)], ws_recv.at[me], v_ss, v_rs, (dp, to)).start()
        if half == 0:
            dx_recv[at_me] = dx_send[0:PAIR]
            ws_recv[me] = ws_send[0]

    gx_out = pltpu.make_async_copy(gx, gx_h, o_sem.at[0])

    def combine():
        drain(dx_send.at[0 : PAIR * (LANES - 1)], b_rs)
        drain(ws_send.at[0 : LANES - 1], v_rs)
        for half, table in enumerate((place_l, place_r)):
            turned = table[...].astype(F32).T.astype(BF)
            for c in range(2):
                at = 1024 * half + 512 * c
                gx[:, at : at + 512] = dot(turned, dx_recv[:, 512 * c : 512 * c + 512]).astype(BF)
        gx_out.start()
        chosen = []
        for s in range(LANES):
            column = jnp.sum(
                jnp.where(diagonal, ws_recv[s, 0:1, :], 0.0), axis=1, keepdims=True
            )
            one = place_l[PAIR * s : PAIR * s + PAIR].astype(F32)[0:CAP]
            chosen.append(jnp.sum(one * column, axis=0, keepdims=True))
        chosen = jnp.concatenate(chosen, axis=0)
        parts = [
            jnp.sum(jnp.where(ids_t[k : k + 1, :] == ex, chosen, 0.0), axis=0, keepdims=True)
            for k in range(8)
        ]
        gw[...] = (jnp.concatenate(parts, axis=0) / rw_t).astype(BF)
        drain(dx_send.at[0 : PAIR * (LANES - 1)], b_ss)
        drain(ws_send.at[0 : LANES - 1], v_ss)

    value = jnp.zeros((HALF, 1), F32)
    for i, k in enumerate(NEAR):
        dispatch(k).wait_recv()
        forward(k)
        if i == LANES // 2 - 2:
            unpack(0)
        if 0 <= i - LANES // 2 + 1 < CHUNKS:
            value = value + hidden_chunk(0, i - LANES // 2 + 1)
        if i == LANES // 2 - 1 + CHUNKS:
            back_rows(0, value)
    back_start(0)
    unpack(1)
    value = hidden_chunk(1, 0)
    turn(0)
    for j in range(AHEAD):
        share_start(j)
    for c in range(1, CHUNKS):
        value = value + hidden_chunk(1, c)
        turn(c)
    back_rows(1, value)
    back_start(1)
    for s in range(4):
        if s == 0:
            own = pl.ds(pl.multiple_of(XBLK * x, XBLK), XBLK)
            x4[0], s4[0] = xb[:, own], sb[:, own]
        else:
            drain(xf.at[s - 1], f_rs.at[s - 1])
            x4[s], s4[s] = split(xf.at[s - 1], slice(None))
    drain(xs_send.at[0 : PAIR * (LANES - 1)], d_ss)
    drain(xf, f_ss)
    for j in range(len(PLAN)):
        if j < PAIRS:
            share_pass(j)
        if 0 < j < PAIRS - AHEAD + 1:
            share_start(j + AHEAD - 1)
        if j < PAIRS:
            share_rest(j)
        for step, *args in PLAN[j]:
            {
                "product": product, "last": z_last, "combine": combine, "out": move_out,
                "pick": move_pick, "in": move_in,
            }[step](*args)
    gx_out.wait()
    for j in range(PAIRS):
        result(j).wait()


def hand_over(*refs):
    sources, results, held, sems = refs[:5], refs[5:10], refs[10:15], refs[15]
    arrive = [
        pltpu.make_async_copy(a, b, sems.at[0, i]) for i, (a, b) in enumerate(zip(sources, held))
    ]
    leave = [
        pltpu.make_async_copy(a, b, sems.at[1, i]) for i, (a, b) in enumerate(zip(held, results))
    ]
    for copy in arrive:
        copy.start()
    for before, after in zip(arrive, leave):
        before.wait()
        after.start()
    for copy in leave:
        copy.wait()


def on_device(
    tokens, cotangent, route_ids, route_weights, capacity, old_owner, new_owner, w_gate, w_up, w_down
):
    vmem = pl.BlockSpec(memory_space=pltpu.VMEM)
    smem = pl.BlockSpec(memory_space=pltpu.SMEM)
    hbm = pl.BlockSpec(memory_space=pl.ANY)
    dma = pltpu.SemaphoreType.DMA
    shard = jax.ShapeDtypeStruct((1, 128, FFN), BF)
    shapes = (
        jax.ShapeDtypeStruct((TOK, D), BF),
        jax.ShapeDtypeStruct((8, TOK), BF),
        shard, shard, shard,
    )
    V = pltpu.VMEM
    parts = pl.pallas_call(
        body,
        out_shape=shapes,
        in_specs=[hbm] * 2 + [vmem] * 4 + [smem] * 2 + [hbm] * 3,
        out_specs=[hbm, vmem, hbm, hbm, hbm],
        scratch_shapes=[
            V((TOK, D), BF), V((TOK, D), BF),
            V((D, FFN), BF), V((D, FFN), BF), V((D, FFN), BF),
            V((2 * ROWS, D), BF), V((2 * ROWS, D), BF), V((3, 2 * ROWS, XBLK), BF),
            V((ROWS, D), BF), V((ROWS, D), BF),
            V((4, ROWS, XBLK), BF), V((4, ROWS, XBLK), BF),
            V((3, ROWS, FFN), BF), V((4, UNITS, 128, ROWS), BF),
            V((UNITS, 4, 128, ZBLK), BF), V((3, UNITS, 128, ZBLK), BF),
            V((2 * ROWS, D // 2), BF), V((2 * ROWS, D // 2), BF),
            V((LANES, 8, 128), F32), V((LANES, 8, 128), F32),
            V((2 * ROWS, TOK), BF), V((2 * ROWS, TOK), BF),
            V((TOK, D), BF),
            V((UNITS, 128, 128), BF),
            V((UNITS, 128, 128), BF),
            V((3, 128, FFN), BF),
            pltpu.SMEM((LANES,), jnp.int32),
            dma((3,)), dma((2,)), dma((1 + PAIRS,)),
            dma, dma((LANES,)), dma, dma((3,)),
            dma((2, UNITS)), dma((2, UNITS)), dma((UNITS,)), dma((UNITS,)),
            dma((3, PAIRS)), dma((3, PAIRS)),
            dma, dma, dma, dma,
            *[dma((len(GROUPS),))] * 4,
            *[V((LANES, count, 16, 128), BF) for _, count in GROUPS + GROUPS],
        ],
        compiler_params=pltpu.CompilerParams(
            collective_id=0, has_side_effects=True, vmem_limit_bytes=62 * 1024 * 1024
        ),
        name="moe",
    )(
        tokens, cotangent, route_ids.T, route_weights.T,
        capacity[None], old_owner[None], old_owner, new_owner,
        w_gate, w_up, w_down,
    )
    grad_x, grad_w, gate, up, down = pl.pallas_call(
        hand_over,
        out_shape=shapes,
        in_specs=[hbm] * 5,
        out_specs=[hbm] * 5,
        scratch_shapes=[V(held.shape, BF) for held in shapes] + [dma((2, 5))],
        compiler_params=pltpu.CompilerParams(vmem_limit_bytes=62 * 1024 * 1024),
        name="results",
    )(*parts)
    return grad_x, grad_w.T, gate, up, down


def solution(mesh):
    rows = P(("dp", "expert"), None)
    slots = P("expert", None, None)
    shards = P("expert", "dp", None)
    return jax.shard_map(
        on_device,
        mesh=mesh,
        in_specs=(rows, rows, rows, rows, P(), P(), P(), slots, slots, slots),
        out_specs=(rows, rows, shards, shards, shards),
        check_vma=False,
    )
```

```python
import math

import jax
import jax.numpy as jnp
from jax import lax
from jax.experimental import pallas as pl
from jax.experimental.pallas import tpu as pltpu
from jax.sharding import PartitionSpec as P

MESH = pl.DeviceIdType.MESH
CAP = 24
LANES = 16
TOK = 256
D = 2048
FFN = 768
ROWS = LANES * CAP
PAIR = 2 * CAP
COLS = 256
CHUNKS = FFN // COLS
UNITS = 6 * CHUNKS
PAIRS = UNITS // 2
AHEAD = 3
GROUPS = ((0, 4), (4, 3), (7, 2))
XBLK = D // 4
ZBLK = XBLK // 4
BF = jnp.bfloat16
F32 = jnp.float32
NT = (((1,), (1,)), ((), ()))


def iota(shape, dim):
    return lax.broadcasted_iota(jnp.int32, shape, dim)


def dot(a, b):
    return jnp.dot(a, b, preferred_element_type=F32)


def dot_nt(a, b):
    return lax.dot_general(a, b, NT, preferred_element_type=F32)


PLAN = (
    (),
    (("product", 0),),
    (("product", 1),),
    (("product", 2), ("last", 0), ("combine",)),
    (("product", 3), ("last", 1)),
    (("product", 4), ("last", 2)),
    (("product", 5), ("last", 3), ("out", 0)),
    (("product", 6), ("last", 4), ("pick", 0)),
    (("product", 7), ("product", 8), ("last", 5), ("in", 0)),
    (
        ("last", 6), ("out", 1), ("last", 7), ("last", 8), ("out", 2),
        ("pick", 1), ("pick", 2), ("in", 1), ("in", 2),
    ),
)


NEAR = (1, 2, 3, 4, 12, 5, 13, 6, 14, 7, 15, 8, 9, 10, 11)
HALF = ROWS // 2


def body(
    tok_h, cot_h, ids, rw, cap, old, old_s, new_s, wg_h, wu_h, wd_h,
    gx_h, gw_h, gg_h, gu_h, gd_h,
    tok, cot, wg, wu, wd, xs_send, xs_recv, xf, xb, sb, x4, s4, hb, ht, zb, zr,
    dx_send, dx_recv, ws_send, ws_recv, place_l, place_r, gx, gw, gbuf, ob, go, wanted,
    w_sem, t_sem, o_sem, d_ss, d_rs, f_ss, f_rs, a_ss, a_rs, g_ss, g_rs, z_ss, z_rs,
    b_ss, b_rs, v_ss, v_rs, p_ss, p_rs, q_ss, q_rs, *moved,
):
    dp = lax.axis_index("dp")
    me = lax.axis_index("expert")
    x, zh = lax.div(dp, 4), lax.rem(dp, 4)
    y, zl, co = lax.div(me, 4), lax.rem(lax.div(me, 2), 2), lax.rem(me, 2)
    p1, p2 = moved[: len(GROUPS)], moved[len(GROUPS) :]

    def at_x(s):
        return (lax.rem(x + (s + 4) % 4, 4) * 4 + zh, me)

    def at_z(s):
        return (x * 4 + lax.rem(zh + (s + 4) % 4, 4), me)

    def ahead(k):
        return lax.rem(y + k // 4, 4) * 4 + lax.rem(zl + (k // 2) % 2, 2) * 2 + lax.rem(co + k % 2, 2)

    def behind(k):
        return lax.rem(y + 4 - k // 4, 4) * 4 + lax.rem(zl + (k // 2) % 2, 2) * 2 + lax.rem(co + k % 2, 2)

    def remote(src, dst, ss, rs, device):
        return pltpu.make_async_remote_copy(
            src_ref=src, dst_ref=dst, send_sem=ss, recv_sem=rs,
            device_id=device, device_id_type=MESH,
        )

    def drain(ref, sem):
        pltpu.make_async_copy(ref, ref, sem).wait()

    rows_in = [
        pltpu.make_async_copy(h, v, t_sem.at[i])
        for i, (h, v) in enumerate(((tok_h, tok), (cot_h, cot)))
    ]
    weights = [
        pltpu.make_async_copy(h.at[0], v, w_sem.at[i])
        for i, (h, v) in enumerate(((wg_h, wg), (wu_h, wu), (wd_h, wd)))
    ]
    for copy in rows_in + weights:
        copy.start()
    barrier = pltpu.get_barrier_semaphore()
    for k in NEAR:
        pl.semaphore_signal(barrier, inc=1, device_id=(dp, ahead(k)), device_id_type=MESH)
    for s in (1, 2, 3):
        pl.semaphore_signal(barrier, inc=1, device_id=at_x(s), device_id_type=MESH)
    for s in (1, 2, 3):
        pl.semaphore_signal(barrier, inc=1, device_id=at_z(s), device_id_type=MESH)

    ids_t = ids[...].astype(F32)
    rw_t = rw[...].astype(F32)
    mine = old[...] == iota((LANES, LANES), 0)
    ex = jnp.sum(jnp.where(mine, iota((LANES, LANES), 1), 0).astype(F32), axis=1, keepdims=True)
    limit = jnp.sum(jnp.where(mine, cap[...], 0).astype(F32), axis=1, keepdims=True)
    named = jnp.zeros((LANES, TOK), F32)
    w_sel = jnp.zeros((LANES, TOK), F32)
    for k in range(8):
        hit = ids_t[k : k + 1, :] == ex
        named = named + jnp.where(hit, 1.0, 0.0)
        w_sel = w_sel + jnp.where(hit, rw_t[k : k + 1, :], 0.0)
    earlier = (iota((TOK, TOK), 0) < iota((TOK, TOK), 1)).astype(F32).astype(BF)
    before = dot(named.astype(BF), earlier)
    pos = jnp.where((named > 0.5) & (before < limit), before, -1.0)
    p_of = iota((CAP, TOK), 0).astype(F32)
    ones = [jnp.where(pos[s : s + 1, :] == p_of, 1.0, 0.0) for s in range(LANES)]
    place = jnp.concatenate(ones, axis=0).astype(BF)
    place_w = jnp.concatenate(
        [one * w_sel[s : s + 1, :] for s, one in enumerate(ones)], axis=0
    ).astype(BF)
    for copy in rows_in:
        copy.wait()
    for c in range(D // 256):
        cols = slice(256 * c, 256 * c + 256)
        rows_x = dot(place, tok[:, cols])
        rows_s = dot(place_w, cot[:, cols])
        both = []
        for s in range(LANES):
            both += [rows_x[CAP * s : CAP * s + CAP], rows_s[CAP * s : CAP * s + CAP]]
        xs_send[:, cols] = jnp.concatenate(both, axis=0).astype(BF)

    pl.semaphore_wait(barrier, LANES - 1 + 6)

    def place_of(k):
        return ((0,) + NEAR).index(k)

    def block(k):
        return pl.ds(PAIR * place_of(k), PAIR)

    def dispatch(k):
        to = ahead(k)
        return remote(
            xs_send.at[pl.ds(pl.multiple_of(PAIR * to, 16), PAIR)], xs_recv.at[block(k)],
            d_ss, d_rs.at[k], (dp, to),
        )

    def columns(s):
        return pl.ds(pl.multiple_of(XBLK * lax.rem(x + s, 4), XBLK), XBLK)

    def forward(k):
        for s in (2, 1, 3):
            remote(
                xs_recv.at[block(k), columns(s)], xf.at[s - 1, block(k)],
                f_ss, f_rs.at[s - 1], at_x(s),
            ).start()

    for k in NEAR:
        dispatch(k).start()
    xs_recv[0:PAIR] = xs_send[pl.ds(pl.multiple_of(PAIR * me, 16), PAIR)]
    forward(0)

    nothing = jnp.zeros((CAP, TOK), F32)
    left, right = [], []
    for one in ones:
        left += [one, nothing]
        right += [nothing, one]
    place_l[...] = jnp.concatenate(left, axis=0).astype(BF)
    place_r[...] = jnp.concatenate(right, axis=0).astype(BF)

    def look_up(j, carry):
        slot = jnp.int32(0)
        for n in range(LANES):
            slot = slot + jnp.where(new_s[n] == j, old_s[n], 0)
        wanted[j] = slot
        return carry

    lax.fori_loop(0, LANES, look_up, 0)
    for copy in weights:
        copy.wait()
    def split(src, cols, first=0, count=LANES):
        both = src[PAIR * first : PAIR * (first + count), cols].astype(F32)
        return [
            jnp.concatenate(
                [both[PAIR * k + at : PAIR * k + at + CAP] for k in range(count)], axis=0
            ).astype(BF)
            for at in (0, CAP)
        ]

    def unpack(half):
        rows = slice(HALF * half, HALF * half + HALF)
        for c in range(D // 256):
            cols = slice(256 * c, 256 * c + 256)
            xb[rows, cols], sb[rows, cols] = split(xs_recv, cols, LANES // 2 * half, LANES // 2)

    def hidden_chunk(half, c):
        rows = slice(HALF * half, HALF * half + HALF)
        cols = slice(COLS * c, COLS * c + COLS)
        gate = dot(xb[rows], wg[:, cols])
        up = dot(xb[rows], wu[:, cols])
        dh = dot(sb[rows], wd[:, cols])
        sig = 1.0 / (1.0 + jnp.exp(-gate))
        act = gate * sig
        hidden = (act * up).astype(BF)
        hb[0, rows, cols] = (dh * up * (sig * (1.0 + gate * (1.0 - sig)))).astype(BF)
        hb[1, rows, cols] = (dh * act).astype(BF)
        hb[2, rows, cols] = hidden
        return jnp.sum(hidden.astype(F32) * dh, axis=1, keepdims=True)

    def turn(c):
        for m in range(3):
            turned = hb[m, :, COLS * c : COLS * c + COLS].astype(F32).T.astype(BF)
            for h in range(2):
                ht[0, 6 * c + 2 * m + h] = turned[128 * h : 128 * h + 128]

    scale = 1.0 / math.sqrt(4 * 4 * LANES * CAP)

    def units_of(j):
        return (2 * j, 2 * j + 1)

    def sign(u):
        return 1 if u % 2 == 0 else -1

    def share(u, s):
        slot = 1 if s == 1 else 3
        return remote(ht.at[0, u], ht.at[slot, u], a_ss.at[slot // 2, u], a_rs.at[slot // 2, u], at_x(s))

    def pass_on(u):
        s = sign(u)
        return remote(ht.at[1 if s == 1 else 3, u], ht.at[2, u], g_ss.at[u], g_rs.at[u], at_x(s))

    def share_start(j):
        up, down = units_of(j)
        share(up, 1).start()
        share(down, -1).start()
        share(down, 1).start()
        share(up, -1).start()

    def share_pass(j):
        for u in units_of(j):
            share(u, sign(u)).wait_recv()
            pass_on(u).start()

    def share_rest(j):
        for u in units_of(j):
            share(u, -sign(u)).wait_recv()

    def z_copy(j, s):
        both = pl.ds(2 * j, 2)
        return remote(
            zb.at[both, lax.rem(zh + s, 4)], zr.at[s - 1, both],
            z_ss.at[s - 1, j], z_rs.at[s - 1, j], at_z(s),
        )

    def product(j):
        rows = s4 if j % 3 == 2 else x4
        up, down = units_of(j)
        total = jnp.zeros((COLS, XBLK), F32)
        for s in (0, 1, 3, 2):
            if s == 2:
                for u in units_of(j):
                    pass_on(u).wait_recv()
            total = total + dot(ht[s, up : down + 1].reshape(COLS, ROWS), rows[s])
        total = (total * scale).astype(BF)
        for h, u in enumerate(units_of(j)):
            for q in range(4):
                zb[u, q] = total[128 * h : 128 * h + 128, ZBLK * q : ZBLK * q + ZBLK]
        for s in (2, 1, 3):
            z_copy(j, s).start()
        for u in units_of(j):
            share(u, 1).wait_send()
            share(u, -1).wait_send()
            pass_on(u).wait_send()

    def z_last(j):
        for s in (1, 3, 2):
            z_copy(j, s).wait_recv()
        for u in units_of(j):
            total = zb[u, zh].astype(F32)
            for s in range(3):
                total = total + zr[s, u].astype(F32)
            gbuf[u] = total.T.astype(BF)
        for s in (1, 3, 2):
            z_copy(j, s).wait_send()

    def piece(g, n):
        first, count = GROUPS[g]
        units = pl.ds(2 * first + count * lax.rem(n, 2), count)
        return units, pl.ds(pl.multiple_of(16 * lax.div(n, 2), 16), 16)

    def move_out(g):
        first, count = GROUPS[g]
        for n in range(LANES):

            @pl.when(n != me)
            def _(n=n):
                at = 2 * first + count * (n % 2)
                part = gbuf.at[at : at + count, 16 * (n // 2) : 16 * (n // 2) + 16]
                remote(part, p1[g].at[me], p_ss.at[g], p_rs.at[g], (dp, n)).start()
        p1[g][me] = gbuf[*piece(g, me)]

    def move_pick(g):
        drain(p1[g].at[0 : LANES - 1], p_rs.at[g])

        def pick(j, carry):
            p2[g][j] = p1[g][wanted[j]]
            return carry

        lax.fori_loop(0, LANES, pick, 0)
        here = ob.at[*piece(g, me)]
        for n in range(LANES):

            @pl.when(n != me)
            def _(n=n):
                remote(p2[g].at[n], here, q_ss.at[g], q_rs.at[g], (dp, n)).start()
        ob[*piece(g, me)] = p2[g][me]
        drain(p1[g].at[0 : LANES - 1], p_ss.at[g])

    def result(j):
        cols = pl.ds(COLS * (j // 3), COLS)
        return pltpu.make_async_copy(
            go.at[j % 3, :, cols], (gg_h, gu_h, gd_h)[j % 3].at[0, :, cols], o_sem.at[2 + j]
        )

    def move_in(g):
        drain(p2[g].at[0 : LANES - 1], q_rs.at[g])
        first, count = GROUPS[g]
        for j in range(first, first + count):
            for h, u in enumerate(units_of(j)):
                at = COLS * (j // 3) + 128 * h
                go[j % 3, :, at : at + 128] = ob[u]
            result(j).start()
        drain(p2[g].at[0 : LANES - 1], q_ss.at[g])

    diagonal = iota((CAP, 128), 0) == iota((CAP, 128), 1)

    def back_rows(half, ws):
        ws = ws / math.sqrt(D)
        rows = slice(HALF * half, HALF * half + HALF)
        for k in range(LANES // 2):
            row = jnp.sum(
                jnp.where(diagonal, ws[CAP * k : CAP * k + CAP], 0.0), axis=0, keepdims=True
            )
            ws_send[LANES // 2 * half + k] = jnp.broadcast_to(row, (8, 128))
        for c in range(4):
            sides = []
            for side in range(2):
                at = 1024 * side + 256 * c
                sides.append(
                    dot_nt(hb[0, rows], wg[at : at + 256, :])
                    + dot_nt(hb[1, rows], wu[at : at + 256, :])
                )
            both = []
            for k in range(LANES // 2):
                both += [part[CAP * k : CAP * k + CAP] for part in sides]
            dx_send[2 * HALF * half : 2 * HALF * (half + 1), 256 * c : 256 * c + 256] = (
                jnp.concatenate(both, axis=0).astype(BF)
            )

    def back_start(half):
        at_me = pl.ds(pl.multiple_of(PAIR * me, 16), PAIR)
        for k in NEAR:
            if place_of(k) // (LANES // 2) != half:
                continue
            to = behind(k)
            remote(dx_send.at[block(k)], dx_recv.at[at_me], b_ss, b_rs, (dp, to)).start()
            remote(ws_send.at[place_of(k)], ws_recv.at[me], v_ss, v_rs, (dp, to)).start()
        if half == 0:
            dx_recv[at_me] = dx_send[0:PAIR]
            ws_recv[me] = ws_send[0]

    gx_out = pltpu.make_async_copy(gx, gx_h, o_sem.at[0])
    gw_out = pltpu.make_async_copy(gw, gw_h, o_sem.at[1])

    def combine():
        drain(dx_send.at[0 : PAIR * (LANES - 1)], b_rs)
        drain(ws_send.at[0 : LANES - 1], v_rs)
        for half, table in enumerate((place_l, place_r)):
            turned = table[...].astype(F32).T.astype(BF)
            for c in range(2):
                at = 1024 * half + 512 * c
                gx[:, at : at + 512] = dot(turned, dx_recv[:, 512 * c : 512 * c + 512]).astype(BF)
        gx_out.start()
        chosen = []
        for s in range(LANES):
            column = jnp.sum(
                jnp.where(diagonal, ws_recv[s, 0:1, :], 0.0), axis=1, keepdims=True
            )
            one = place_l[PAIR * s : PAIR * s + PAIR].astype(F32)[0:CAP]
            chosen.append(jnp.sum(one * column, axis=0, keepdims=True))
        chosen = jnp.concatenate(chosen, axis=0)
        parts = [
            jnp.sum(jnp.where(ids_t[k : k + 1, :] == ex, chosen, 0.0), axis=0, keepdims=True)
            for k in range(8)
        ]
        gw[...] = (jnp.concatenate(parts, axis=0) / rw_t).astype(BF)
        gw_out.start()
        drain(dx_send.at[0 : PAIR * (LANES - 1)], b_ss)
        drain(ws_send.at[0 : LANES - 1], v_ss)

    value = jnp.zeros((HALF, 1), F32)
    for i, k in enumerate(NEAR):
        dispatch(k).wait_recv()
        forward(k)
        if i == LANES // 2 - 2:
            unpack(0)
        if 0 <= i - LANES // 2 + 1 < CHUNKS:
            value = value + hidden_chunk(0, i - LANES // 2 + 1)
        if i == LANES // 2 - 1 + CHUNKS:
            back_rows(0, value)
    back_start(0)
    unpack(1)
    value = hidden_chunk(1, 0)
    turn(0)
    for j in range(AHEAD):
        share_start(j)
    for c in range(1, CHUNKS):
        value = value + hidden_chunk(1, c)
        turn(c)
    back_rows(1, value)
    back_start(1)
    for s in range(4):
        if s == 0:
            own = pl.ds(pl.multiple_of(XBLK * x, XBLK), XBLK)
            x4[0], s4[0] = xb[:, own], sb[:, own]
        else:
            drain(xf.at[s - 1], f_rs.at[s - 1])
            x4[s], s4[s] = split(xf.at[s - 1], slice(None))
    drain(xs_send.at[0 : PAIR * (LANES - 1)], d_ss)
    drain(xf, f_ss)
    for j in range(len(PLAN)):
        if j < PAIRS:
            share_pass(j)
        if 0 < j < PAIRS - AHEAD + 1:
            share_start(j + AHEAD - 1)
        if j < PAIRS:
            share_rest(j)
        for step, *args in PLAN[j]:
            {
                "product": product, "last": z_last, "combine": combine, "out": move_out,
                "pick": move_pick, "in": move_in,
            }[step](*args)
    gx_out.wait()
    gw_out.wait()
    for j in range(PAIRS):
        result(j).wait()


def hand_over(*refs):
    sources, results, held, sems = refs[:5], refs[5:10], refs[10:15], refs[15]
    arrive = [
        pltpu.make_async_copy(a, b, sems.at[0, i]) for i, (a, b) in enumerate(zip(sources, held))
    ]
    leave = [
        pltpu.make_async_copy(a, b, sems.at[1, i]) for i, (a, b) in enumerate(zip(held, results))
    ]
    for copy in arrive:
        copy.start()
    for before, after in zip(arrive, leave):
        before.wait()
        after.start()
    for copy in leave:
        copy.wait()


def on_device(
    tokens, cotangent, route_ids, route_weights, capacity, old_owner, new_owner, w_gate, w_up, w_down
):
    vmem = pl.BlockSpec(memory_space=pltpu.VMEM)
    smem = pl.BlockSpec(memory_space=pltpu.SMEM)
    hbm = pl.BlockSpec(memory_space=pl.ANY)
    dma = pltpu.SemaphoreType.DMA
    shard = jax.ShapeDtypeStruct((1, 128, FFN), BF)
    shapes = (
        jax.ShapeDtypeStruct((TOK, D), BF),
        jax.ShapeDtypeStruct((8, TOK), BF),
        shard, shard, shard,
    )
    V = pltpu.VMEM
    parts = pl.pallas_call(
        body,
        out_shape=shapes,
        in_specs=[hbm] * 2 + [vmem] * 4 + [smem] * 2 + [hbm] * 3,
        out_specs=[hbm] * 5,
        scratch_shapes=[
            V((TOK, D), BF), V((TOK, D), BF),
            V((D, FFN), BF), V((D, FFN), BF), V((D, FFN), BF),
            V((2 * ROWS, D), BF), V((2 * ROWS, D), BF), V((3, 2 * ROWS, XBLK), BF),
            V((ROWS, D), BF), V((ROWS, D), BF),
            V((4, ROWS, XBLK), BF), V((4, ROWS, XBLK), BF),
            V((3, ROWS, FFN), BF), V((4, UNITS, 128, ROWS), BF),
            V((UNITS, 4, 128, ZBLK), BF), V((3, UNITS, 128, ZBLK), BF),
            V((2 * ROWS, D // 2), BF), V((2 * ROWS, D // 2), BF),
            V((LANES, 8, 128), F32), V((LANES, 8, 128), F32),
            V((2 * ROWS, TOK), BF), V((2 * ROWS, TOK), BF),
            V((TOK, D), BF), V((8, TOK), BF),
            V((UNITS, 128, 128), BF),
            V((UNITS, 128, 128), BF),
            V((3, 128, FFN), BF),
            pltpu.SMEM((LANES,), jnp.int32),
            dma((3,)), dma((2,)), dma((2 + PAIRS,)),
            dma, dma((LANES,)), dma, dma((3,)),
            dma((2, UNITS)), dma((2, UNITS)), dma((UNITS,)), dma((UNITS,)),
            dma((3, PAIRS)), dma((3, PAIRS)),
            dma, dma, dma, dma,
            *[dma((len(GROUPS),))] * 4,
            *[V((LANES, count, 16, 128), BF) for _, count in GROUPS + GROUPS],
        ],
        compiler_params=pltpu.CompilerParams(
            collective_id=0, has_side_effects=True, vmem_limit_bytes=62 * 1024 * 1024
        ),
        name="moe",
    )(
        tokens, cotangent, route_ids.T, route_weights.T,
        capacity[None], old_owner[None], old_owner, new_owner,
        w_gate, w_up, w_down,
    )
    grad_x, grad_w, gate, up, down = pl.pallas_call(
        hand_over,
        out_shape=shapes,
        in_specs=[hbm] * 5,
        out_specs=[hbm] * 5,
        scratch_shapes=[V(held.shape, BF) for held in shapes] + [dma((2, 5))],
        compiler_params=pltpu.CompilerParams(vmem_limit_bytes=62 * 1024 * 1024),
        name="results",
    )(*parts)
    return grad_x, grad_w.T, gate, up, down


def solution(mesh):
    rows = P(("dp", "expert"), None)
    slots = P("expert", None, None)
    shards = P("expert", "dp", None)
    return jax.shard_map(
        on_device,
        mesh=mesh,
        in_specs=(rows, rows, rows, rows, P(), P(), P(), slots, slots, slots),
        out_specs=(rows, rows, shards, shards, shards),
        check_vma=False,
    )
```

```python
import math

import jax
import jax.numpy as jnp
from jax import lax
from jax.experimental import pallas as pl
from jax.experimental.pallas import tpu as pltpu
from jax.sharding import PartitionSpec as P

MESH = pl.DeviceIdType.MESH
CAP = 24
LANES = 16
TOK = 256
D = 2048
FFN = 768
ROWS = LANES * CAP
PAIR = 2 * CAP
COLS = 256
CHUNKS = FFN // COLS
UNITS = 6 * CHUNKS
PAIRS = UNITS // 2
AHEAD = 3
GROUPS = ((0, 6), (6, 3))
XBLK = D // 4
ZBLK = XBLK // 4
BF = jnp.bfloat16
F32 = jnp.float32
NT = (((1,), (1,)), ((), ()))


def iota(shape, dim):
    return lax.broadcasted_iota(jnp.int32, shape, dim)


def dot(a, b):
    return jnp.dot(a, b, preferred_element_type=F32)


def dot_nt(a, b):
    return lax.dot_general(a, b, NT, preferred_element_type=F32)


PLAN = (
    (),
    (("product", 0),),
    (("product", 1),),
    (("product", 2), ("last", 0), ("combine",)),
    (("product", 3), ("last", 1)),
    (("product", 4), ("last", 2)),
    (("product", 5), ("last", 3)),
    (("product", 6), ("last", 4)),
    (("product", 7), ("product", 8), ("last", 5), ("out", 0)),
    (
        ("last", 6), ("last", 7), ("last", 8), ("out", 1),
        ("pick", 0), ("pick", 1), ("in", 0), ("in", 1),
    ),
)


NEAR = (1, 2, 3, 4, 12, 5, 13, 6, 14, 7, 15, 8, 9, 10, 11)
HALF = ROWS // 2


def body(
    tok_h, cot_h, ids, rw, cap, old, old_s, new_s, wg_h, wu_h, wd_h,
    gx_h, gw_h, gg_h, gu_h, gd_h,
    tok, cot, wg, wu, wd, xs_send, xs_recv, xf, xb, sb, x4, s4, hb, ht, zb, zr,
    dx_send, dx_recv, ws_send, ws_recv, place_l, place_r, gx, gw, gbuf, ob, go, wanted,
    w_sem, t_sem, o_sem, d_ss, d_rs, f_ss, f_rs, a_ss, a_rs, g_ss, g_rs, z_ss, z_rs,
    b_ss, b_rs, v_ss, v_rs, p_ss, p_rs, q_ss, q_rs, *moved,
):
    dp = lax.axis_index("dp")
    me = lax.axis_index("expert")
    x, zh = lax.div(dp, 4), lax.rem(dp, 4)
    y, zl, co = lax.div(me, 4), lax.rem(lax.div(me, 2), 2), lax.rem(me, 2)
    p1, p2 = moved[: len(GROUPS)], moved[len(GROUPS) :]

    def at_x(s):
        return (lax.rem(x + (s + 4) % 4, 4) * 4 + zh, me)

    def at_z(s):
        return (x * 4 + lax.rem(zh + (s + 4) % 4, 4), me)

    def ahead(k):
        return lax.rem(y + k // 4, 4) * 4 + lax.rem(zl + (k // 2) % 2, 2) * 2 + lax.rem(co + k % 2, 2)

    def behind(k):
        return lax.rem(y + 4 - k // 4, 4) * 4 + lax.rem(zl + (k // 2) % 2, 2) * 2 + lax.rem(co + k % 2, 2)

    def remote(src, dst, ss, rs, device):
        return pltpu.make_async_remote_copy(
            src_ref=src, dst_ref=dst, send_sem=ss, recv_sem=rs,
            device_id=device, device_id_type=MESH,
        )

    def drain(ref, sem):
        pltpu.make_async_copy(ref, ref, sem).wait()

    rows_in = [
        pltpu.make_async_copy(h, v, t_sem.at[i])
        for i, (h, v) in enumerate(((tok_h, tok), (cot_h, cot)))
    ]
    weights = [
        pltpu.make_async_copy(h.at[0], v, w_sem.at[i])
        for i, (h, v) in enumerate(((wg_h, wg), (wu_h, wu), (wd_h, wd)))
    ]
    for copy in rows_in + weights:
        copy.start()
    barrier = pltpu.get_barrier_semaphore()
    for k in NEAR:
        pl.semaphore_signal(barrier, inc=1, device_id=(dp, ahead(k)), device_id_type=MESH)
    for s in (1, 2, 3):
        pl.semaphore_signal(barrier, inc=1, device_id=at_x(s), device_id_type=MESH)
    for s in (1, 2, 3):
        pl.semaphore_signal(barrier, inc=1, device_id=at_z(s), device_id_type=MESH)

    ids_t = ids[...].astype(F32)
    rw_t = rw[...].astype(F32)
    mine = old[...] == iota((LANES, LANES), 0)
    ex = jnp.sum(jnp.where(mine, iota((LANES, LANES), 1), 0).astype(F32), axis=1, keepdims=True)
    limit = jnp.sum(jnp.where(mine, cap[...], 0).astype(F32), axis=1, keepdims=True)
    named = jnp.zeros((LANES, TOK), F32)
    w_sel = jnp.zeros((LANES, TOK), F32)
    for k in range(8):
        hit = ids_t[k : k + 1, :] == ex
        named = named + jnp.where(hit, 1.0, 0.0)
        w_sel = w_sel + jnp.where(hit, rw_t[k : k + 1, :], 0.0)
    earlier = (iota((TOK, TOK), 0) < iota((TOK, TOK), 1)).astype(F32).astype(BF)
    before = dot(named.astype(BF), earlier)
    pos = jnp.where((named > 0.5) & (before < limit), before, -1.0)
    p_of = iota((CAP, TOK), 0).astype(F32)
    ones = [jnp.where(pos[s : s + 1, :] == p_of, 1.0, 0.0) for s in range(LANES)]
    place = jnp.concatenate(ones, axis=0).astype(BF)
    place_w = jnp.concatenate(
        [one * w_sel[s : s + 1, :] for s, one in enumerate(ones)], axis=0
    ).astype(BF)
    for copy in rows_in:
        copy.wait()
    for c in range(D // 256):
        cols = slice(256 * c, 256 * c + 256)
        rows_x = dot(place, tok[:, cols])
        rows_s = dot(place_w, cot[:, cols])
        both = []
        for s in range(LANES):
            both += [rows_x[CAP * s : CAP * s + CAP], rows_s[CAP * s : CAP * s + CAP]]
        xs_send[:, cols] = jnp.concatenate(both, axis=0).astype(BF)

    pl.semaphore_wait(barrier, LANES - 1 + 6)

    def place_of(k):
        return ((0,) + NEAR).index(k)

    def block(k):
        return pl.ds(PAIR * place_of(k), PAIR)

    def dispatch(k):
        to = ahead(k)
        return remote(
            xs_send.at[pl.ds(pl.multiple_of(PAIR * to, 16), PAIR)], xs_recv.at[block(k)],
            d_ss, d_rs.at[k], (dp, to),
        )

    def columns(s):
        return pl.ds(pl.multiple_of(XBLK * lax.rem(x + s, 4), XBLK), XBLK)

    def forward(k):
        for s in (2, 1, 3):
            remote(
                xs_recv.at[block(k), columns(s)], xf.at[s - 1, block(k)],
                f_ss, f_rs.at[s - 1], at_x(s),
            ).start()

    for k in NEAR:
        dispatch(k).start()
    xs_recv[0:PAIR] = xs_send[pl.ds(pl.multiple_of(PAIR * me, 16), PAIR)]
    forward(0)

    nothing = jnp.zeros((CAP, TOK), F32)
    left, right = [], []
    for one in ones:
        left += [one, nothing]
        right += [nothing, one]
    place_l[...] = jnp.concatenate(left, axis=0).astype(BF)
    place_r[...] = jnp.concatenate(right, axis=0).astype(BF)

    def look_up(j, carry):
        slot = jnp.int32(0)
        for n in range(LANES):
            slot = slot + jnp.where(new_s[n] == j, old_s[n], 0)
        wanted[j] = slot
        return carry

    lax.fori_loop(0, LANES, look_up, 0)
    for copy in weights:
        copy.wait()
    def split(src, cols, first=0, count=LANES):
        both = src[PAIR * first : PAIR * (first + count), cols].astype(F32)
        return [
            jnp.concatenate(
                [both[PAIR * k + at : PAIR * k + at + CAP] for k in range(count)], axis=0
            ).astype(BF)
            for at in (0, CAP)
        ]

    def unpack(half):
        rows = slice(HALF * half, HALF * half + HALF)
        for c in range(D // 256):
            cols = slice(256 * c, 256 * c + 256)
            xb[rows, cols], sb[rows, cols] = split(xs_recv, cols, LANES // 2 * half, LANES // 2)

    def hidden_chunk(half, c):
        rows = slice(HALF * half, HALF * half + HALF)
        cols = slice(COLS * c, COLS * c + COLS)
        gate = dot(xb[rows], wg[:, cols])
        up = dot(xb[rows], wu[:, cols])
        dh = dot(sb[rows], wd[:, cols])
        sig = 1.0 / (1.0 + jnp.exp(-gate))
        act = gate * sig
        hidden = (act * up).astype(BF)
        hb[0, rows, cols] = (dh * up * (sig * (1.0 + gate * (1.0 - sig)))).astype(BF)
        hb[1, rows, cols] = (dh * act).astype(BF)
        hb[2, rows, cols] = hidden
        return jnp.sum(hidden.astype(F32) * dh, axis=1, keepdims=True)

    def turn(c):
        for m in range(3):
            turned = hb[m, :, COLS * c : COLS * c + COLS].astype(F32).T.astype(BF)
            for h in range(2):
                ht[0, 6 * c + 2 * m + h] = turned[128 * h : 128 * h + 128]

    scale = 1.0 / math.sqrt(4 * 4 * LANES * CAP)

    def units_of(j):
        return (2 * j, 2 * j + 1)

    def sign(u):
        return 1 if u % 2 == 0 else -1

    def share(u, s):
        slot = 1 if s == 1 else 3
        return remote(ht.at[0, u], ht.at[slot, u], a_ss.at[slot // 2, u], a_rs.at[slot // 2, u], at_x(s))

    def pass_on(u):
        s = sign(u)
        return remote(ht.at[1 if s == 1 else 3, u], ht.at[2, u], g_ss.at[u], g_rs.at[u], at_x(s))

    def share_start(j):
        up, down = units_of(j)
        share(up, 1).start()
        share(down, -1).start()
        share(down, 1).start()
        share(up, -1).start()

    def share_pass(j):
        for u in units_of(j):
            share(u, sign(u)).wait_recv()
            pass_on(u).start()

    def share_rest(j):
        for u in units_of(j):
            share(u, -sign(u)).wait_recv()

    def z_copy(j, s):
        both = pl.ds(2 * j, 2)
        return remote(
            zb.at[both, lax.rem(zh + s, 4)], zr.at[s - 1, both],
            z_ss.at[s - 1, j], z_rs.at[s - 1, j], at_z(s),
        )

    def product(j):
        rows = s4 if j % 3 == 2 else x4
        up, down = units_of(j)
        total = jnp.zeros((COLS, XBLK), F32)
        for s in (0, 1, 3, 2):
            if s == 2:
                for u in units_of(j):
                    pass_on(u).wait_recv()
            total = total + dot(ht[s, up : down + 1].reshape(COLS, ROWS), rows[s])
        total = (total * scale).astype(BF)
        for h, u in enumerate(units_of(j)):
            for q in range(4):
                zb[u, q] = total[128 * h : 128 * h + 128, ZBLK * q : ZBLK * q + ZBLK]
        for s in (2, 1, 3):
            z_copy(j, s).start()
        for u in units_of(j):
            share(u, 1).wait_send()
            share(u, -1).wait_send()
            pass_on(u).wait_send()

    def z_last(j):
        for s in (1, 3, 2):
            z_copy(j, s).wait_recv()
        for u in units_of(j):
            total = zb[u, zh].astype(F32)
            for s in range(3):
                total = total + zr[s, u].astype(F32)
            gbuf[u] = total.T.astype(BF)
        for s in (1, 3, 2):
            z_copy(j, s).wait_send()

    def piece(g, n):
        first, count = GROUPS[g]
        units = pl.ds(2 * first + count * lax.rem(n, 2), count)
        return units, pl.ds(pl.multiple_of(16 * lax.div(n, 2), 16), 16)

    def move_out(g):
        first, count = GROUPS[g]
        for n in range(LANES):

            @pl.when(n != me)
            def _(n=n):
                at = 2 * first + count * (n % 2)
                part = gbuf.at[at : at + count, 16 * (n // 2) : 16 * (n // 2) + 16]
                remote(part, p1[g].at[me], p_ss.at[g], p_rs.at[g], (dp, n)).start()
        p1[g][me] = gbuf[*piece(g, me)]

    def move_pick(g):
        drain(p1[g].at[0 : LANES - 1], p_rs.at[g])

        def pick(j, carry):
            p2[g][j] = p1[g][wanted[j]]
            return carry

        lax.fori_loop(0, LANES, pick, 0)
        here = ob.at[*piece(g, me)]
        for n in range(LANES):

            @pl.when(n != me)
            def _(n=n):
                remote(p2[g].at[n], here, q_ss.at[g], q_rs.at[g], (dp, n)).start()
        ob[*piece(g, me)] = p2[g][me]
        drain(p1[g].at[0 : LANES - 1], p_ss.at[g])

    def result(j):
        cols = pl.ds(COLS * (j // 3), COLS)
        return pltpu.make_async_copy(
            go.at[j % 3, :, cols], (gg_h, gu_h, gd_h)[j % 3].at[0, :, cols], o_sem.at[2 + j]
        )

    def move_in(g):
        drain(p2[g].at[0 : LANES - 1], q_rs.at[g])
        first, count = GROUPS[g]
        for j in range(first, first + count):
            for h, u in enumerate(units_of(j)):
                at = COLS * (j // 3) + 128 * h
                go[j % 3, :, at : at + 128] = ob[u]
            result(j).start()
        drain(p2[g].at[0 : LANES - 1], q_ss.at[g])

    diagonal = iota((CAP, 128), 0) == iota((CAP, 128), 1)

    def back_rows(half, ws):
        ws = ws / math.sqrt(D)
        rows = slice(HALF * half, HALF * half + HALF)
        for k in range(LANES // 2):
            row = jnp.sum(
                jnp.where(diagonal, ws[CAP * k : CAP * k + CAP], 0.0), axis=0, keepdims=True
            )
            ws_send[LANES // 2 * half + k] = jnp.broadcast_to(row, (8, 128))
        for c in range(4):
            sides = []
            for side in range(2):
                at = 1024 * side + 256 * c
                sides.append(
                    dot_nt(hb[0, rows], wg[at : at + 256, :])
                    + dot_nt(hb[1, rows], wu[at : at + 256, :])
                )
            both = []
            for k in range(LANES // 2):
                both += [part[CAP * k : CAP * k + CAP] for part in sides]
            dx_send[2 * HALF * half : 2 * HALF * (half + 1), 256 * c : 256 * c + 256] = (
                jnp.concatenate(both, axis=0).astype(BF)
            )

    def back_start(half):
        at_me = pl.ds(pl.multiple_of(PAIR * me, 16), PAIR)
        for k in NEAR:
            if place_of(k) // (LANES // 2) != half:
                continue
            to = behind(k)
            remote(dx_send.at[block(k)], dx_recv.at[at_me], b_ss, b_rs, (dp, to)).start()
            remote(ws_send.at[place_of(k)], ws_recv.at[me], v_ss, v_rs, (dp, to)).start()
        if half == 0:
            dx_recv[at_me] = dx_send[0:PAIR]
            ws_recv[me] = ws_send[0]

    gx_out = pltpu.make_async_copy(gx, gx_h, o_sem.at[0])
    gw_out = pltpu.make_async_copy(gw, gw_h, o_sem.at[1])

    def combine():
        drain(dx_send.at[0 : PAIR * (LANES - 1)], b_rs)
        drain(ws_send.at[0 : LANES - 1], v_rs)
        for half, table in enumerate((place_l, place_r)):
            turned = table[...].astype(F32).T.astype(BF)
            for c in range(2):
                at = 1024 * half + 512 * c
                gx[:, at : at + 512] = dot(turned, dx_recv[:, 512 * c : 512 * c + 512]).astype(BF)
        gx_out.start()
        chosen = []
        for s in range(LANES):
            column = jnp.sum(
                jnp.where(diagonal, ws_recv[s, 0:1, :], 0.0), axis=1, keepdims=True
            )
            one = place_l[PAIR * s : PAIR * s + PAIR].astype(F32)[0:CAP]
            chosen.append(jnp.sum(one * column, axis=0, keepdims=True))
        chosen = jnp.concatenate(chosen, axis=0)
        parts = [
            jnp.sum(jnp.where(ids_t[k : k + 1, :] == ex, chosen, 0.0), axis=0, keepdims=True)
            for k in range(8)
        ]
        gw[...] = (jnp.concatenate(parts, axis=0) / rw_t).astype(BF)
        gw_out.start()
        drain(dx_send.at[0 : PAIR * (LANES - 1)], b_ss)
        drain(ws_send.at[0 : LANES - 1], v_ss)

    value = jnp.zeros((HALF, 1), F32)
    for i, k in enumerate(NEAR):
        dispatch(k).wait_recv()
        forward(k)
        if i == LANES // 2 - 2:
            unpack(0)
        if 0 <= i - LANES // 2 + 1 < CHUNKS:
            value = value + hidden_chunk(0, i - LANES // 2 + 1)
        if i == LANES // 2 - 1 + CHUNKS:
            back_rows(0, value)
    back_start(0)
    unpack(1)
    value = hidden_chunk(1, 0)
    turn(0)
    for j in range(AHEAD):
        share_start(j)
    for c in range(1, CHUNKS):
        value = value + hidden_chunk(1, c)
        turn(c)
    back_rows(1, value)
    back_start(1)
    for s in range(4):
        if s == 0:
            own = pl.ds(pl.multiple_of(XBLK * x, XBLK), XBLK)
            x4[0], s4[0] = xb[:, own], sb[:, own]
        else:
            drain(xf.at[s - 1], f_rs.at[s - 1])
            x4[s], s4[s] = split(xf.at[s - 1], slice(None))
    drain(xs_send.at[0 : PAIR * (LANES - 1)], d_ss)
    drain(xf, f_ss)
    for j in range(len(PLAN)):
        if j < PAIRS:
            share_pass(j)
        if 0 < j < PAIRS - AHEAD + 1:
            share_start(j + AHEAD - 1)
        if j < PAIRS:
            share_rest(j)
        for step, *args in PLAN[j]:
            {
                "product": product, "last": z_last, "combine": combine, "out": move_out,
                "pick": move_pick, "in": move_in,
            }[step](*args)
    gx_out.wait()
    gw_out.wait()
    for j in range(PAIRS):
        result(j).wait()


def hand_over(*refs):
    sources, results, held, sems = refs[:5], refs[5:10], refs[10:15], refs[15]
    arrive = [
        pltpu.make_async_copy(a, b, sems.at[0, i]) for i, (a, b) in enumerate(zip(sources, held))
    ]
    leave = [
        pltpu.make_async_copy(a, b, sems.at[1, i]) for i, (a, b) in enumerate(zip(held, results))
    ]
    for copy in arrive:
        copy.start()
    for before, after in zip(arrive, leave):
        before.wait()
        after.start()
    for copy in leave:
        copy.wait()


def on_device(
    tokens, cotangent, route_ids, route_weights, capacity, old_owner, new_owner, w_gate, w_up, w_down
):
    vmem = pl.BlockSpec(memory_space=pltpu.VMEM)
    smem = pl.BlockSpec(memory_space=pltpu.SMEM)
    hbm = pl.BlockSpec(memory_space=pl.ANY)
    dma = pltpu.SemaphoreType.DMA
    shard = jax.ShapeDtypeStruct((1, 128, FFN), BF)
    shapes = (
        jax.ShapeDtypeStruct((TOK, D), BF),
        jax.ShapeDtypeStruct((8, TOK), BF),
        shard, shard, shard,
    )
    V = pltpu.VMEM
    parts = pl.pallas_call(
        body,
        out_shape=shapes,
        in_specs=[hbm] * 2 + [vmem] * 4 + [smem] * 2 + [hbm] * 3,
        out_specs=[hbm] * 5,
        scratch_shapes=[
            V((TOK, D), BF), V((TOK, D), BF),
            V((D, FFN), BF), V((D, FFN), BF), V((D, FFN), BF),
            V((2 * ROWS, D), BF), V((2 * ROWS, D), BF), V((3, 2 * ROWS, XBLK), BF),
            V((ROWS, D), BF), V((ROWS, D), BF),
            V((4, ROWS, XBLK), BF), V((4, ROWS, XBLK), BF),
            V((3, ROWS, FFN), BF), V((4, UNITS, 128, ROWS), BF),
            V((UNITS, 4, 128, ZBLK), BF), V((3, UNITS, 128, ZBLK), BF),
            V((2 * ROWS, D // 2), BF), V((2 * ROWS, D // 2), BF),
            V((LANES, 8, 128), F32), V((LANES, 8, 128), F32),
            V((2 * ROWS, TOK), BF), V((2 * ROWS, TOK), BF),
            V((TOK, D), BF), V((8, TOK), BF),
            V((UNITS, 128, 128), BF),
            V((UNITS, 128, 128), BF),
            V((3, 128, FFN), BF),
            pltpu.SMEM((LANES,), jnp.int32),
            dma((3,)), dma((2,)), dma((2 + PAIRS,)),
            dma, dma((LANES,)), dma, dma((3,)),
            dma((2, UNITS)), dma((2, UNITS)), dma((UNITS,)), dma((UNITS,)),
            dma((3, PAIRS)), dma((3, PAIRS)),
            dma, dma, dma, dma,
            *[dma((len(GROUPS),))] * 4,
            *[V((LANES, count, 16, 128), BF) for _, count in GROUPS + GROUPS],
        ],
        compiler_params=pltpu.CompilerParams(
            collective_id=0, has_side_effects=True, vmem_limit_bytes=62 * 1024 * 1024
        ),
        name="moe",
    )(
        tokens, cotangent, route_ids.T, route_weights.T,
        capacity[None], old_owner[None], old_owner, new_owner,
        w_gate, w_up, w_down,
    )
    grad_x, grad_w, gate, up, down = pl.pallas_call(
        hand_over,
        out_shape=shapes,
        in_specs=[hbm] * 5,
        out_specs=[hbm] * 5,
        scratch_shapes=[V(held.shape, BF) for held in shapes] + [dma((2, 5))],
        compiler_params=pltpu.CompilerParams(vmem_limit_bytes=62 * 1024 * 1024),
        name="results",
    )(*parts)
    return grad_x, grad_w.T, gate, up, down


def solution(mesh):
    rows = P(("dp", "expert"), None)
    slots = P("expert", None, None)
    shards = P("expert", "dp", None)
    return jax.shard_map(
        on_device,
        mesh=mesh,
        in_specs=(rows, rows, rows, rows, P(), P(), P(), slots, slots, slots),
        out_specs=(rows, rows, shards, shards, shards),
        check_vma=False,
    )
```
